32 devices in a mesh: groups: 2 (over x), attn: 8 (over z, y), expert: 2 (over core).
Axes of the slice: x: 2, y: 2, z: 4, core: 2. Of those that a mesh axis runs over, the one named last changes fastest.
Arguments:
- hidden_in: bfloat16 [512, 6144], P(('groups', 'attn', 'expert')), parts along dimension 0, may hold values from -6 to 6
- queries: bfloat16 [512, 6144], P(('groups', 'attn', 'expert')), parts along dimension 0, may hold values from -60 to 60
- cache_keys: bfloat16 [512, 64, 1024], P(('groups', 'attn', 'expert')), parts along dimension 0, may hold values from -4 to 4
- cache_values: bfloat16 [512, 64, 1024], P(('groups', 'attn', 'expert')), parts along dimension 0, may hold values from -6 to 6
- new_keys: bfloat16 [512, 1024], P(('groups', 'attn', 'expert')), parts along dimension 0, may hold values from -6 to 6
- new_values: bfloat16 [512, 1024], P(('groups', 'attn', 'expert')), parts along dimension 0, may hold values from -6 to 6
- lengths: int32 [512], P(('groups', 'attn', 'expert')), parts along dimension 0, may hold values from 2 to 64
- expert_ids: int32 [512, 4], P(('groups', 'attn', 'expert')), parts along dimension 0, may hold values from 0 to 15, as said below
- gate_probs: float32 [512, 4], P(('groups', 'attn', 'expert')), parts along dimension 0, may hold values from 0.05 to 1
- w_gate: bfloat16 [2, 6144, 6144], P('expert', None, 'attn'), may hold values from -0.078125 to 0.078125
- w_up: bfloat16 [2, 6144, 6144], P('expert', None, 'attn'), may hold values from -0.078125 to 0.078125
- w_down: bfloat16 [2, 6144, 6144], P('expert', 'attn'), may hold values from -0.078125 to 0.078125
Outputs:
- stream: float32 [512, 6144], P(('groups', 'attn', 'expert')), parts along dimension 0
The draws below stay inside these ranges and needn't reach their ends.
There are 2 independent parts, one for each index of `groups`. The reference program is written for one: setup_inputs(seed, part) draws one part's arguments, and reference() takes and returns one part's arrays. A program takes and returns all parts, laid end to end along the dimension named above; an argument that names none is the same for every part. Nothing has to cross between parts.
Inputs may be any that keep to these rules, and one draw needn't show every extreme that they name: `expert_ids`: each request names 4 different experts. Among the 16 requests of one device exactly 8 name expert 0 and 1 to 8 name expert 1, exactly 8 on some device.
All inputs are finite; a program needn't handle non-finite values.
Results may differ from the reference program's by a relative error of at most 0.0019.
Values may be sent and summed in bfloat16 or wider, within the bound.
No kernel may reach another device: no remote copies, remote signals or barrier semaphores. Data moves between devices by JAX's collectives and lax.ppermute only.
A program may use at most 128 MiB of HBM per device.

```python
import math
import jax
import jax.numpy as jnp
from jax import lax

D = 6144
HEADS = 48
KV_HEADS = 8
HEAD = 128
EXPERTS = 16
TOP = 4
FFW = 6144
CACHE_LEN = 64
REQ_DEV = 16
CAP = 8
EXP_WIN = 2
REQS = 256


def shared_cache(key, weight):
    shape = (REQS, CACHE_LEN, KV_HEADS * HEAD)
    normal_part = jnp.clip(jax.random.normal(jax.random.fold_in(key, 2), shape, jnp.float32), -4.0, 4.0)
    blended = normal_part
    picked = (jax.random.randint(jax.random.fold_in(key, 3), (REQS,), 0, 8) == 0) & (weight > 0.5)
    levels = jax.random.randint(jax.random.fold_in(key, 4), (REQS,), 1, 4).astype(jnp.float32)
    leading = blended[:, 0, :]
    shrink = 1.0 - 2.0 / (10.0 * levels * math.sqrt(HEAD))
    second = jnp.where(picked[:, None], leading * shrink[:, None], blended[:, 1, :])
    blended = blended.at[:, 1, :].set(second)
    return blended


def draw_cache_keys(key, part):
    blended = shared_cache(key, 0.0)
    return blended.astype(jnp.bfloat16)


def draw_queries(key, part):
    own_key = jax.random.fold_in(key, 21)
    result = jnp.clip(jax.random.normal(own_key, (REQS, HEADS * HEAD), jnp.float32), -4.0, 4.0)
    return result.astype(jnp.bfloat16)


def draw_expert_ids(key, part):
    key = jax.random.fold_in(key, 5)
    blocks = REQS // REQ_DEV
    row_keys = jax.random.split(jax.random.fold_in(key, 1), REQS)
    others = jax.vmap(lambda row_key: jax.random.permutation(row_key, EXPERTS - 2))(row_keys)[:, :TOP] + 2
    order_zero = jax.vmap(lambda row_key: jax.random.permutation(row_key, REQ_DEV))(jax.random.split(jax.random.fold_in(key, 2), blocks))
    order_one = jax.vmap(lambda row_key: jax.random.permutation(row_key, REQ_DEV))(jax.random.split(jax.random.fold_in(key, 3), blocks))
    count_one = jax.random.randint(jax.random.fold_in(key, 4), (blocks,), 1, CAP + 1)
    full_block = jax.random.randint(jax.random.fold_in(key, 5), (), 0, blocks)
    count_one = jnp.where(jnp.arange(blocks) == full_block, CAP, count_one)
    has_zero = (order_zero < CAP).reshape(REQS)
    has_one = (order_one < count_one[:, None]).reshape(REQS)
    first_col = jnp.where(has_zero, 0, others[:, 0])
    second_col = jnp.where(has_one, 1, others[:, 1])
    id_table = jnp.concatenate([first_col[:, None], second_col[:, None], others[:, 2:]], 1)
    rotation = jax.random.randint(jax.random.fold_in(key, 6), (REQS,), 0, TOP)
    columns = (jnp.arange(TOP)[None, :] + rotation[:, None]) % TOP
    return jnp.take_along_axis(id_table, columns, 1).astype(jnp.int32)


def set_ends(values, key, smallest, largest):
    index_at = [jax.random.randint(jax.random.fold_in(key, axis), (), 0, length) for axis, length in enumerate(values.shape)]
    widest = values.shape.index(max(values.shape))
    next_to = index_at[:widest] + [(index_at[widest] + 1) % values.shape[widest]] + index_at[widest + 1:]
    return values.at[tuple(index_at)].set(smallest).at[tuple(next_to)].set(largest)


def level_of(key, shape, pieces, low, largest):
    level = 1.0
    for dim, blocks in pieces:
        steps = jax.random.uniform(jax.random.fold_in(jax.random.fold_in(key, 6), dim), (blocks,), jnp.float32, low / len(pieces), largest / len(pieces))
        level = level * jnp.repeat(jnp.exp(steps), shape[dim] // blocks).reshape((-1,) + (1,) * (len(shape) - 1 - dim))
    return level


def gaussian(key, extent, deviation, most, cuts=(), kind=jnp.bfloat16):
    factor_of = level_of(key, extent, cuts, -0.22, 0.18) if cuts else 1.0
    drawn = jax.random.normal(key, extent, jnp.float32) * deviation * factor_of
    return jnp.minimum(jnp.maximum(drawn, -most), most).astype(kind)


def setup_inputs(seed: int = 0, part: int = 0) -> dict:
    seeds = jax.random.split(jax.random.key(seed), 13)
    part_keys = jax.random.split(jax.random.fold_in(seeds[12], part), 13)
    return {
        "hidden_in": gaussian(part_keys[0], (REQS, D), 1.0, 6.0, ((0, 16),)),
        "queries": draw_queries(jax.random.fold_in(jax.random.fold_in(seeds[12], part), 71), part),
        "cache_keys": draw_cache_keys(jax.random.fold_in(jax.random.fold_in(seeds[12], part), 71), part),
        "cache_values": gaussian(part_keys[3], (REQS, CACHE_LEN, KV_HEADS * HEAD), 1.0, 6.0, ((0, 16),)),
        "new_keys": gaussian(part_keys[4], (REQS, KV_HEADS * HEAD), 1.0, 6.0, ((0, 16),)),
        "new_values": gaussian(part_keys[5], (REQS, KV_HEADS * HEAD), 1.0, 6.0, ((0, 16),)),
        "lengths": set_ends(jax.random.randint(part_keys[6], (REQS,), 2, CACHE_LEN + 1), jax.random.fold_in(part_keys[6], 1), 2, CACHE_LEN).astype(jnp.int32),
        "expert_ids": draw_expert_ids(jax.random.fold_in(jax.random.fold_in(seeds[12], part), 71), part),
        "gate_probs": jnp.clip(jnp.exp(math.log(1.0) - 2.9957323 * jax.random.uniform(part_keys[8], (REQS, TOP), jnp.float32) ** level_of(part_keys[8], (REQS, TOP), ((0, 16),), -0.2, 0.2)), 0.05, 1.0),
        "w_gate": gaussian(seeds[9], (EXP_WIN, D, FFW), D ** -0.5, 0.078125, ((0, 2), (2, 8))),
        "w_up": gaussian(seeds[10], (EXP_WIN, D, FFW), D ** -0.5, 0.078125, ((0, 2), (2, 8))),
        "w_down": gaussian(seeds[11], (EXP_WIN, FFW, D), FFW ** -0.5, 0.078125, ((0, 2), (1, 8))),
    }


def attend(queries, cache_keys, cache_values, new_keys, new_values, lengths):
    count = queries.shape[0]
    cache_span = cache_keys.shape[1]
    kv_heads = cache_keys.shape[2] // HEAD
    group_size = queries.shape[1] // cache_keys.shape[2]
    query_heads = queries.astype(jnp.float32).reshape(count, kv_heads, group_size, HEAD)
    key_cache = cache_keys.astype(jnp.float32).reshape(count, cache_span, kv_heads, HEAD)
    val_cache = cache_values.astype(jnp.float32).reshape(count, cache_span, kv_heads, HEAD)
    own_keys = new_keys.astype(jnp.float32).reshape(count, kv_heads, HEAD)
    own_values = new_values.astype(jnp.float32).reshape(count, kv_heads, HEAD)
    score_scale = 1.0 / math.sqrt(HEAD)
    cached = jnp.einsum('rgjd,rpgd->rgjp', query_heads, key_cache) * score_scale
    valid_mask = (jnp.arange(cache_span, dtype=jnp.int32)[None, :] < lengths[:, None])[:, None, None, :]
    cached = jnp.where(valid_mask, cached, -1e+30)
    own_score = jnp.einsum('rgjd,rgd->rgj', query_heads, own_keys) * score_scale
    top_score = jnp.maximum(lax.optimization_barrier(jnp.max(cached, -1)), own_score)
    cached_exp = jnp.where(valid_mask, jnp.exp(cached - top_score[..., None]), 0.0)
    own_exp = jnp.exp(own_score - top_score)
    denom_sum = lax.optimization_barrier(jnp.sum(cached_exp, -1)) + own_exp
    weights_cache = (cached_exp / denom_sum[..., None]).astype(jnp.bfloat16)
    weights_own = (own_exp / denom_sum).astype(jnp.bfloat16)
    mixed = jnp.einsum('rgjp,rpgd->rgjd', weights_cache.astype(jnp.float32), val_cache)
    mixed = mixed + weights_own.astype(jnp.float32)[..., None] * own_values[:, :, None, :]
    return mixed.reshape(count, -1)

def reference(hidden_in, queries, cache_keys, cache_values, new_keys, new_values, lengths, expert_ids, gate_probs, w_gate, w_up, w_down):
    residual = hidden_in.astype(jnp.float32) + attend(queries, cache_keys, cache_values, new_keys, new_values, lengths)
    centre = lax.optimization_barrier(jnp.mean(residual, -1, keepdims=True))
    centered = residual - centre
    variance = lax.optimization_barrier(jnp.mean(centered * centered, -1, keepdims=True))
    normed = (centered * lax.rsqrt(variance + 1e-05)).astype(jnp.bfloat16)
    mix_weights = gate_probs / lax.optimization_barrier(jnp.sum(gate_probs, -1, keepdims=True))
    stream = residual
    for expert in range(EXP_WIN):
        gate_act = jnp.dot(normed, w_gate[expert], preferred_element_type=jnp.float32)
        upward = jnp.dot(normed, w_up[expert], preferred_element_type=jnp.float32)
        gated = (jax.nn.silu(gate_act) * upward).astype(jnp.bfloat16)
        expert_out = jnp.dot(gated, w_down[expert], preferred_element_type=jnp.float32)
        coefficient = lax.optimization_barrier(jnp.sum(jnp.where(expert_ids == expert, mix_weights, 0.0), -1))
        stream = stream + coefficient[:, None] * expert_out
    return stream
```

```python
import math

import jax
import jax.numpy as jnp
from jax import lax
from jax.sharding import PartitionSpec as P

HEAD = 128


def ring_of(count):
    if count == 8:
        return [0, 2, 4, 6, 7, 5, 3, 1]
    return list(range(count))


def body(
    hidden_in,
    queries,
    cache_keys,
    cache_values,
    new_keys,
    new_values,
    lengths,
    expert_ids,
    gate_probs,
    w_gate,
    w_up,
    w_down,
):
    row_count = hidden_in.shape[0]
    feat_width = hidden_in.shape[1]
    cache_span = cache_keys.shape[1]
    kv_width = cache_keys.shape[2]
    kv_heads = kv_width // HEAD
    group_size = queries.shape[1] // kv_width
    score_scale = 1.0 / math.sqrt(HEAD)
    query_heads = queries.reshape(row_count, kv_heads, group_size, HEAD)
    key_cache = cache_keys.reshape(row_count, cache_span, kv_heads, HEAD)
    val_cache = cache_values.reshape(row_count, cache_span, kv_heads, HEAD)
    cached = (
        jnp.einsum("rgjd,rpgd->rgjp", query_heads, key_cache, preferred_element_type=jnp.float32)
        * score_scale
    )
    valid_mask = (jnp.arange(cache_span, dtype=jnp.int32)[None, :] < lengths[:, None])[
        :, None, None, :
    ]
    cached = jnp.where(valid_mask, cached, -1e30)
    own_score = (
        jnp.einsum(
            "rgjd,rgd->rgj",
            query_heads,
            new_keys.reshape(row_count, kv_heads, HEAD),
            preferred_element_type=jnp.float32,
        )
        * score_scale
    )
    top_score = jnp.maximum(jnp.max(cached, -1), own_score)
    cached_exp = jnp.where(valid_mask, jnp.exp(cached - top_score[..., None]), 0.0)
    own_exp = jnp.exp(own_score - top_score)
    denom_sum = jnp.sum(cached_exp, -1) + own_exp
    weights_cache = (cached_exp / denom_sum[..., None]).astype(jnp.bfloat16)
    weights_own = (own_exp / denom_sum).astype(jnp.bfloat16)
    mixed = jnp.einsum(
        "rgjp,rpgd->rgjd", weights_cache, val_cache, preferred_element_type=jnp.float32
    )
    own_values = new_values.astype(jnp.float32).reshape(row_count, kv_heads, 1, HEAD)
    mixed = mixed + weights_own.astype(jnp.float32)[..., None] * own_values
    residual = hidden_in.astype(jnp.float32) + mixed.reshape(row_count, feat_width)
    centre = jnp.mean(residual, -1, keepdims=True)
    centered = residual - centre
    variance = jnp.mean(centered * centered, -1, keepdims=True)
    normed = (centered * lax.rsqrt(variance + 1e-05)).astype(jnp.bfloat16)
    mix_weights = gate_probs / jnp.sum(gate_probs, -1, keepdims=True)

    here = lax.axis_index("expert")
    labels = jnp.stack([here, 1 - here]).astype(jnp.int32)
    matches = expert_ids[None, :, :] == labels[:, None, None]
    coefficient = jnp.sum(jnp.where(matches, mix_weights[None], 0.0), -1)
    chosen = jnp.any(matches, -1)
    earlier = jnp.arange(row_count)[:, None] > jnp.arange(row_count)[None, :]
    slot_rank = jnp.sum(jnp.where(earlier[None], chosen[:, None, :], False).astype(jnp.int32), -1)
    cap_slots = row_count // 2
    selector = (
        slot_rank[:, None, :] == jnp.arange(cap_slots, dtype=jnp.int32)[None, :, None]
    ) & chosen[:, None, :]
    outgoing = jnp.einsum(
        "ejr,rd->ejd", selector.astype(jnp.bfloat16), normed, preferred_element_type=jnp.float32
    ).astype(jnp.bfloat16)

    count = lax.axis_size("attn")
    ring = ring_of(count)
    right = [(ring[i], ring[(i + 1) % count]) for i in range(count)]
    left = [(b, a) for a, b in right]
    swap = [(0, 1), (1, 0)]

    def go_right(block):
        return lax.ppermute(block, "attn", right)

    def go_left(block):
        return lax.ppermute(block, "attn", left)

    half = count // 2
    own = outgoing[0]
    theirs = lax.ppermute(outgoing[1], "expert", swap)
    own_r, own_l, theirs_r, theirs_l = [own], [own], [theirs], [theirs]
    for step in range(1, half + 1):
        own_r.append(go_right(own_r[-1]))
        theirs_l.append(go_left(theirs_l[-1]))
        if step < half:
            own_l.append(go_left(own_l[-1]))
            theirs_r.append(go_right(theirs_r[-1]))

    def experts(rows):
        gate_act = jnp.dot(rows, w_gate[0], preferred_element_type=jnp.float32)
        upward = jnp.dot(rows, w_up[0], preferred_element_type=jnp.float32)
        hidden_act = (jax.nn.silu(gate_act) * upward).astype(jnp.bfloat16)
        return jnp.dot(hidden_act, w_down[0], preferred_element_type=jnp.float32)

    blocks = [own, theirs]
    for step in range(1, half):
        blocks += [own_r[step], own_l[step], theirs_r[step], theirs_l[step]]
    blocks += [own_r[half], theirs_l[half]]
    share = experts(jnp.concatenate(blocks)).reshape(len(blocks), cap_slots, feat_width)
    own_share = {0: share[0], half: share[-2]}
    theirs_share = {0: share[1], -half: share[-1]}
    for step in range(1, half):
        at = 4 * step - 2
        own_share[-step], own_share[step] = share[at], share[at + 1]
        theirs_share[-step], theirs_share[step] = share[at + 2], share[at + 3]

    def narrow(block):
        return block.astype(jnp.bfloat16)

    own_from_l = narrow(own_share[half])
    theirs_from_r = narrow(theirs_share[-half])
    own_from_r = narrow(own_share[1 - half])
    theirs_from_l = narrow(theirs_share[half - 1])
    for step in range(half - 1, 0, -1):
        own_from_l = narrow(go_right(own_from_l).astype(jnp.float32) + own_share[step])
        theirs_from_r = narrow(go_left(theirs_from_r).astype(jnp.float32) + theirs_share[-step])
        if step > 1:
            own_from_r = narrow(
                go_left(own_from_r).astype(jnp.float32) + own_share[1 - step]
            )
            theirs_from_l = narrow(
                go_right(theirs_from_l).astype(jnp.float32) + theirs_share[step - 1]
            )
    own_total = (
        own_share[0]
        + go_right(own_from_l).astype(jnp.float32)
        + go_left(own_from_r).astype(jnp.float32)
    )
    theirs_total = (
        theirs_share[0]
        + go_left(theirs_from_r).astype(jnp.float32)
        + go_right(theirs_from_l).astype(jnp.float32)
    )
    back = lax.ppermute(narrow(theirs_total), "expert", swap).astype(jnp.float32)
    returned = jnp.stack([own_total, back])
    weighted = selector.astype(jnp.float32) * coefficient[:, None, :]
    expert_sum = jnp.einsum("ejr,ejd->rd", weighted, returned, precision=lax.Precision.HIGHEST)
    return residual + expert_sum


def solution(mesh):
    placed = (
        P(("groups", "attn", "expert"), None),
        P(("groups", "attn", "expert"), None),
        P(("groups", "attn", "expert"), None, None),
        P(("groups", "attn", "expert"), None, None),
        P(("groups", "attn", "expert"), None),
        P(("groups", "attn", "expert"), None),
        P(("groups", "attn", "expert")),
        P(("groups", "attn", "expert"), None),
        P(("groups", "attn", "expert"), None),
        P("expert", None, "attn"),
        P("expert", None, "attn"),
        P("expert", "attn", None),
    )
    return jax.shard_map(
        body,
        mesh=mesh,
        in_specs=placed,
        out_specs=P(("groups", "attn", "expert"), None),
        check_vma=False,
    )
```

```python
import math

import jax
import jax.numpy as jnp
from jax import lax
from jax.experimental import pallas as pl
from jax.experimental.pallas import tpu as pltpu
from jax.sharding import PartitionSpec as P

HEAD = 128


def ring_of(count):
    if count == 8:
        return [0, 2, 4, 6, 7, 5, 3, 1]
    return list(range(count))


def experts_kernel(rows_ref, gate_ref, up_ref, down_ref, out_ref, act_ref):
    feat_width = rows_ref.shape[1]
    hidden = gate_ref.shape[1]
    step = 256

    @pl.loop(0, hidden // step)
    def _(index):
        columns = pl.ds(pl.multiple_of(index * step, step), step)
        gate_act = jnp.dot(
            rows_ref[...], gate_ref[:, columns], preferred_element_type=jnp.float32
        )
        upward = jnp.dot(rows_ref[...], up_ref[:, columns], preferred_element_type=jnp.float32)
        act_ref[:, columns] = (gate_act / (1.0 + jnp.exp(-gate_act)) * upward).astype(
            act_ref.dtype
        )

    wide = 512

    @pl.loop(0, feat_width // wide)
    def _(index):
        columns = pl.ds(pl.multiple_of(index * wide, wide), wide)
        out_ref[:, columns] = jnp.dot(
            act_ref[...], down_ref[:, columns], preferred_element_type=jnp.float32
        ).astype(out_ref.dtype)


def experts(rows, gate, up, down):
    count, feat_width = rows.shape
    hidden = gate.shape[1]
    vmem = pl.BlockSpec(memory_space=pltpu.VMEM)
    return pl.pallas_call(
        experts_kernel,
        out_shape=jax.ShapeDtypeStruct((count, feat_width), jnp.bfloat16),
        in_specs=[vmem] * 4,
        out_specs=vmem,
        scratch_shapes=[pltpu.VMEM((count, hidden), jnp.bfloat16)],
        compiler_params=pltpu.CompilerParams(vmem_limit_bytes=8 << 20),
        cost_estimate=pl.CostEstimate(
            flops=6 * count * feat_width * hidden,
            bytes_accessed=6 * feat_width * hidden,
            transcendentals=count * hidden,
        ),
    )(rows, gate, up, down)


def add_kernel(*refs):
    total = refs[0][...].astype(jnp.float32)
    for ref in refs[1:-1]:
        total = total + ref[...].astype(jnp.float32)
    refs[-1][...] = total.astype(refs[-1].dtype)


def add(*terms):
    vmem = pl.BlockSpec(memory_space=pltpu.VMEM)
    size = terms[0].size
    return pl.pallas_call(
        add_kernel,
        out_shape=jax.ShapeDtypeStruct(terms[0].shape, terms[0].dtype),
        in_specs=[vmem] * len(terms),
        out_specs=vmem,
        compiler_params=pltpu.CompilerParams(vmem_limit_bytes=1 << 20),
        cost_estimate=pl.CostEstimate(
            flops=size * len(terms), bytes_accessed=2 * size * len(terms), transcendentals=0
        ),
    )(*terms)


def front_kernel(
    here_ref,
    hidden_ref,
    query_ref,
    key_ref,
    value_ref,
    new_key_ref,
    new_value_ref,
    length_ref,
    ids_ref,
    probs_ref,
    residual_ref,
    own_ref,
    theirs_ref,
    slots_ref,
    weights_ref,
    normed_ref,
):
    rows, feat_width = hidden_ref.shape
    span = key_ref.shape[1]
    kv_width = key_ref.shape[2]
    kv_heads = kv_width // HEAD
    group = feat_width // kv_width
    scale = 1.0 / math.sqrt(HEAD)
    shape = (group * rows, rows * span)
    column = lax.broadcasted_iota(jnp.int32, shape, 1)
    request = lax.broadcasted_iota(jnp.int32, shape, 0) & (rows - 1)
    first = request * span
    limit = first + jnp.concatenate([length_ref[...]] * group, 0)
    valid = (column >= first) & (column < limit)
    total = jnp.zeros((rows, 1), jnp.float32)
    for head in range(kv_heads):
        lanes = pl.ds(head * HEAD, HEAD)
        wanted = [head * group + member for member in range(group)]
        query = jnp.concatenate([query_ref[:, q * HEAD : (q + 1) * HEAD] for q in wanted], 0)
        keys = key_ref[:, :, lanes].reshape(rows * span, HEAD)
        scores = (
            lax.dot_general(
                query, keys, (((1,), (1,)), ((), ())), preferred_element_type=jnp.float32
            )
            * scale
        )
        scores = jnp.where(valid, scores, -1e30)
        new_key = jnp.concatenate([new_key_ref[:, lanes].astype(jnp.float32)] * group, 0)
        own_score = jnp.sum(query.astype(jnp.float32) * new_key, -1, keepdims=True) * scale
        top = jnp.maximum(jnp.max(scores, -1, keepdims=True), own_score)
        powers = jnp.exp(scores - top)
        own_power = jnp.exp(own_score - top)
        inverse = 1.0 / (jnp.sum(powers, -1, keepdims=True) + own_power)
        attention = (powers * inverse).astype(jnp.bfloat16)
        own_weight = (own_power * inverse).astype(jnp.bfloat16).astype(jnp.float32)
        values = value_ref[:, :, lanes].reshape(rows * span, HEAD)
        mixed = jnp.dot(attention, values, preferred_element_type=jnp.float32)
        new_value = jnp.concatenate([new_value_ref[:, lanes].astype(jnp.float32)] * group, 0)
        mixed = mixed + own_weight * new_value
        for member, q in enumerate(wanted):
            cols = pl.ds(q * HEAD, HEAD)
            part = hidden_ref[:, cols].astype(jnp.float32) + mixed[
                member * rows : (member + 1) * rows
            ]
            residual_ref[:, cols] = part
            total = total + jnp.sum(part, -1, keepdims=True)
    centre = total * (1.0 / feat_width)
    spread = jnp.zeros((rows, 1), jnp.float32)
    wide = 1024
    for at in range(0, feat_width, wide):
        centered = residual_ref[:, at : at + wide] - centre
        spread = spread + jnp.sum(centered * centered, -1, keepdims=True)
    inverse = lax.rsqrt(spread * (1.0 / feat_width) + 1e-05)
    for at in range(0, feat_width, wide):
        centered = residual_ref[:, at : at + wide] - centre
        normed_ref[:, at : at + wide] = (centered * inverse).astype(jnp.bfloat16)

    here = here_ref[0]
    mix = probs_ref[...] / jnp.sum(probs_ref[...], -1, keepdims=True)
    below = (
        lax.broadcasted_iota(jnp.int32, (rows, rows), 0)
        > lax.broadcasted_iota(jnp.int32, (rows, rows), 1)
    ).astype(jnp.float32)
    cap = own_ref.shape[0]
    slot = lax.broadcasted_iota(jnp.int32, (rows, cap), 1).astype(jnp.float32)
    for place, label in enumerate((here, 1 - here)):
        match = ids_ref[...] == label
        weights_ref[:, place : place + 1] = jnp.sum(jnp.where(match, mix, 0.0), -1, keepdims=True)
        chosen = jnp.max(jnp.where(match, 1.0, 0.0), -1, keepdims=True)
        rank = jnp.dot(
            below, jnp.broadcast_to(chosen, (rows, cap)), preferred_element_type=jnp.float32
        )
        picks = jnp.where(rank == slot, chosen, 0.0)
        slots_ref[:, place * cap : (place + 1) * cap] = picks
        out_ref = (own_ref, theirs_ref)[place]
        out_ref[...] = lax.dot_general(
            picks.astype(jnp.bfloat16),
            normed_ref[...],
            (((0,), (0,)), ((), ())),
            preferred_element_type=jnp.float32,
        ).astype(jnp.bfloat16)


def tail_kernel(
    residual_ref, slots_ref, weights_ref, first_ref, second_ref, third_ref, back_ref, out_ref
):
    cap = back_ref.shape[0]
    own = (
        first_ref[...].astype(jnp.float32)
        + second_ref[...].astype(jnp.float32)
        + third_ref[...].astype(jnp.float32)
    ).astype(jnp.bfloat16)
    result = residual_ref[...]
    for place, block in enumerate((own, back_ref[...])):
        picks = slots_ref[:, place * cap : (place + 1) * cap].astype(jnp.bfloat16)
        result = result + weights_ref[:, place : place + 1] * jnp.dot(
            picks, block, preferred_element_type=jnp.float32
        )
    out_ref[...] = result


def body(
    hidden_in,
    queries,
    cache_keys,
    cache_values,
    new_keys,
    new_values,
    lengths,
    expert_ids,
    gate_probs,
    w_gate,
    w_up,
    w_down,
):
    row_count = hidden_in.shape[0]
    feat_width = hidden_in.shape[1]
    cap_slots = row_count // 2
    vmem = pl.BlockSpec(memory_space=pltpu.VMEM)
    here = lax.axis_index("expert").astype(jnp.int32).reshape(1)
    residual, own, theirs, slots, weights = pl.pallas_call(
        front_kernel,
        out_shape=(
            jax.ShapeDtypeStruct((row_count, feat_width), jnp.float32),
            jax.ShapeDtypeStruct((cap_slots, feat_width), jnp.bfloat16),
            jax.ShapeDtypeStruct((cap_slots, feat_width), jnp.bfloat16),
            jax.ShapeDtypeStruct((row_count, 2 * cap_slots), jnp.float32),
            jax.ShapeDtypeStruct((row_count, 2), jnp.float32),
        ),
        in_specs=[pl.BlockSpec(memory_space=pltpu.SMEM)] + [vmem] * 9,
        out_specs=(vmem,) * 5,
        scratch_shapes=[pltpu.VMEM((row_count, feat_width), jnp.bfloat16)],
        compiler_params=pltpu.CompilerParams(vmem_limit_bytes=16 << 20),
        cost_estimate=pl.CostEstimate(
            flops=10**9, bytes_accessed=40 * 10**6, transcendentals=10**6
        ),
    )(
        here,
        hidden_in,
        queries,
        cache_keys,
        cache_values,
        new_keys,
        new_values,
        lengths.reshape(row_count, 1),
        expert_ids,
        gate_probs,
    )

    count = lax.axis_size("attn")
    ring = ring_of(count)
    right = [(ring[i], ring[(i + 1) % count]) for i in range(count)]
    left = [(b, a) for a, b in right]
    swap = [(0, 1), (1, 0)]

    def go_right(block):
        return lax.ppermute(block, "attn", right)

    def go_left(block):
        return lax.ppermute(block, "attn", left)

    half = count // 2
    theirs = lax.ppermute(theirs, "expert", swap)
    own_r, own_l, theirs_r, theirs_l = [own], [own], [theirs], [theirs]
    for step in range(1, half + 1):
        own_r.append(go_right(own_r[-1]))
        theirs_l.append(go_left(theirs_l[-1]))
        if step < half:
            own_l.append(go_left(own_l[-1]))
            theirs_r.append(go_right(theirs_r[-1]))

    blocks = [own, theirs]
    for step in range(1, half):
        blocks += [own_r[step], own_l[step], theirs_r[step], theirs_l[step]]
    blocks += [own_r[half], theirs_l[half]]
    share = experts(jnp.concatenate(blocks), w_gate[0], w_up[0], w_down[0]).reshape(len(blocks), cap_slots, feat_width)
    own_share = {0: share[0], half: share[-2]}
    theirs_share = {0: share[1], -half: share[-1]}
    for step in range(1, half):
        at = 4 * step - 2
        own_share[-step], own_share[step] = share[at], share[at + 1]
        theirs_share[-step], theirs_share[step] = share[at + 2], share[at + 3]

    own_from_l = own_share[half]
    theirs_from_r = theirs_share[-half]
    own_from_r = own_share[1 - half]
    theirs_from_l = theirs_share[half - 1]
    for step in range(half - 1, 0, -1):
        own_from_l = add(go_right(own_from_l), own_share[step])
        theirs_from_r = add(go_left(theirs_from_r), theirs_share[-step])
        if step > 1:
            own_from_r = add(go_left(own_from_r), own_share[1 - step])
            theirs_from_l = add(go_right(theirs_from_l), theirs_share[step - 1])
    theirs_total = add(
        theirs_share[0], go_left(theirs_from_r), go_right(theirs_from_l)
    )
    back = lax.ppermute(theirs_total, "expert", swap)
    return pl.pallas_call(
        tail_kernel,
        out_shape=jax.ShapeDtypeStruct((row_count, feat_width), jnp.float32),
        in_specs=[vmem] * 7,
        out_specs=vmem,
        compiler_params=pltpu.CompilerParams(vmem_limit_bytes=4 << 20),
    )(
        residual,
        slots,
        weights,
        own_share[0],
        go_right(own_from_l),
        go_left(own_from_r),
        back,
    )


def solution(mesh):
    placed = (
        P(("groups", "attn", "expert"), None),
        P(("groups", "attn", "expert"), None),
        P(("groups", "attn", "expert"), None, None),
        P(("groups", "attn", "expert"), None, None),
        P(("groups", "attn", "expert"), None),
        P(("groups", "attn", "expert"), None),
        P(("groups", "attn", "expert")),
        P(("groups", "attn", "expert"), None),
        P(("groups", "attn", "expert"), None),
        P("expert", None, "attn"),
        P("expert", None, "attn"),
        P("expert", "attn", None),
    )
    return jax.shard_map(
        body,
        mesh=mesh,
        in_specs=placed,
        out_specs=P(("groups", "attn", "expert"), None),
        check_vma=False,
    )
```

```python
import math

import jax
import jax.numpy as jnp
from jax import lax
from jax.experimental import pallas as pl
from jax.experimental.pallas import tpu as pltpu
from jax.sharding import PartitionSpec as P

HEAD = 128


def ring_of(count):
    if count == 8:
        return [0, 2, 4, 6, 7, 5, 3, 1]
    return list(range(count))


def load_kernel(after_ref, source_ref, held_ref, sem):
    copy = pltpu.make_async_copy(source_ref, held_ref, sem)
    copy.start()
    copy.wait()


def in_hbm(array):
    return pltpu.with_memory_space_constraint(array, pltpu.HBM)


def load(weights, after, room):
    return pl.pallas_call(
        load_kernel,
        out_shape=pltpu.VMEM(weights.shape, weights.dtype),
        in_specs=[pl.BlockSpec(memory_space=pl.ANY), pl.BlockSpec(memory_space=pltpu.HBM)],
        out_specs=pl.BlockSpec(memory_space=pltpu.VMEM),
        scratch_shapes=[pltpu.SemaphoreType.DMA],
        compiler_params=pltpu.CompilerParams(vmem_limit_bytes=room),
        cost_estimate=pl.CostEstimate(
            flops=0, bytes_accessed=2 * weights.size, transcendentals=0
        ),
    )(after, in_hbm(weights))


def experts_kernel(rows_ref, gate_ref, up_ref, down_ref, out_ref, act_ref):
    feat_width = rows_ref.shape[1]
    hidden = gate_ref.shape[1]
    step = math.gcd(hidden, 256)
    for at in range(0, hidden, step):
        gate_act = jnp.dot(
            rows_ref[...], gate_ref[:, at : at + step], preferred_element_type=jnp.float32
        )
        upward = jnp.dot(
            rows_ref[...], up_ref[:, at : at + step], preferred_element_type=jnp.float32
        )
        act_ref[:, at : at + step] = (gate_act / (1.0 + jnp.exp(-gate_act)) * upward).astype(
            act_ref.dtype
        )
    wide = 512
    for at in range(0, feat_width, wide):
        out_ref[:, at : at + wide] = jnp.dot(
            act_ref[...], down_ref[:, at : at + wide], preferred_element_type=jnp.float32
        ).astype(out_ref.dtype)


def experts(rows, gate, up, down):
    count, feat_width = rows.shape
    hidden = gate.shape[1]
    vmem = pl.BlockSpec(memory_space=pltpu.VMEM)
    return pl.pallas_call(
        experts_kernel,
        out_shape=jax.ShapeDtypeStruct((count, feat_width), jnp.bfloat16),
        in_specs=[vmem] * 4,
        out_specs=vmem,
        scratch_shapes=[pltpu.VMEM((count, hidden), jnp.bfloat16)],
        compiler_params=pltpu.CompilerParams(vmem_limit_bytes=8<<20),
        cost_estimate=pl.CostEstimate(
            flops=6 * count * feat_width * hidden,
            bytes_accessed=6 * feat_width * hidden,
            transcendentals=count * hidden,
        ),
    )(rows, gate, up, down)


def add_kernel(*refs):
    total = refs[0][...].astype(jnp.float32)
    for ref in refs[1:-1]:
        total = total + ref[...].astype(jnp.float32)
    refs[-1][...] = total.astype(refs[-1].dtype)


def add(*terms):
    vmem = pl.BlockSpec(memory_space=pltpu.VMEM)
    size = terms[0].size
    return pl.pallas_call(
        add_kernel,
        out_shape=jax.ShapeDtypeStruct(terms[0].shape, terms[0].dtype),
        in_specs=[vmem] * len(terms),
        out_specs=vmem,
        compiler_params=pltpu.CompilerParams(vmem_limit_bytes=1 << 20),
        cost_estimate=pl.CostEstimate(
            flops=size * len(terms), bytes_accessed=2 * size * len(terms), transcendentals=0
        ),
    )(*terms)


def column_of(row):
    shape = (row.shape[1], row.shape[1])
    same = lax.broadcasted_iota(jnp.int32, shape, 0) == lax.broadcasted_iota(jnp.int32, shape, 1)
    return jnp.sum(jnp.where(same, row, 0.0), -1, keepdims=True)


def front_kernel(
    here_ref,
    hidden_hbm,
    query_hbm,
    key_hbm,
    value_hbm,
    new_key_hbm,
    new_value_hbm,
    length_hbm,
    ids_hbm,
    probs_hbm,
    gate_hbm,
    residual_ref,
    own_ref,
    theirs_ref,
    slots_ref,
    weights_ref,
    gate_ref,
    hidden_ref,
    query_ref,
    key_ref,
    value_ref,
    new_key_ref,
    new_value_ref,
    length_ref,
    ids_ref,
    probs_ref,
    normed_ref,
    sems,
):
    half = key_ref.shape[2] // 2
    low, high = pl.ds(0, half), pl.ds(half, half)
    pairs = [
        (length_hbm, length_ref),
        (query_hbm, query_ref),
        (key_hbm.at[:, :, low], key_ref.at[:, :, low]),
        (new_key_hbm, new_key_ref),
        (value_hbm.at[:, :, low], value_ref.at[:, :, low]),
        (new_value_hbm, new_value_ref),
        (hidden_hbm, hidden_ref),
        (key_hbm.at[:, :, high], key_ref.at[:, :, high]),
        (value_hbm.at[:, :, high], value_ref.at[:, :, high]),
        (ids_hbm, ids_ref),
        (probs_hbm, probs_ref),
        (gate_hbm, gate_ref),
    ]
    copies = [
        pltpu.make_async_copy(source, target, sems.at[at])
        for at, (source, target) in enumerate(pairs)
    ]
    for copy in copies[:-1]:
        copy.start()
    for copy in copies[:4]:
        copy.wait()
    copies[-1].start()
    rows, feat_width = hidden_ref.shape
    span = key_ref.shape[1]
    kv_width = key_ref.shape[2]
    kv_heads = kv_width // HEAD
    group = feat_width // kv_width
    scale = 1.0 / math.sqrt(HEAD)
    shape = (group * rows, rows * span)
    column = lax.broadcasted_iota(jnp.int32, shape, 1)
    request = lax.broadcasted_iota(jnp.int32, shape, 0) & (rows - 1)
    first = request * span
    lengths = column_of(length_ref[...].astype(jnp.float32)).astype(jnp.int32)
    limit = first + jnp.concatenate([lengths] * group, 0)
    valid = (column >= first) & (column < limit)
    total = jnp.zeros((rows, 1), jnp.float32)
    for head in range(kv_heads):
        if head * 2 == kv_heads:
            copies[7].wait()
            copies[8].wait()
        lanes = pl.ds(head * HEAD, HEAD)
        wanted = [head * group + member for member in range(group)]
        query = jnp.concatenate([query_ref[:, q * HEAD : (q + 1) * HEAD] for q in wanted], 0)
        keys = key_ref[:, :, lanes].reshape(rows * span, HEAD)
        scores = (
            lax.dot_general(
                query, keys, (((1,), (1,)), ((), ())), preferred_element_type=jnp.float32
            )
            * scale
        )
        scores = jnp.where(valid, scores, -1e30)
        new_key = jnp.concatenate([new_key_ref[:, lanes].astype(jnp.float32)] * group, 0)
        own_score = jnp.sum(query.astype(jnp.float32) * new_key, -1, keepdims=True) * scale
        top = jnp.maximum(jnp.max(scores, -1, keepdims=True), own_score)
        powers = jnp.exp(scores - top)
        own_power = jnp.exp(own_score - top)
        inverse = 1.0 / (jnp.sum(powers, -1, keepdims=True) + own_power)
        attention = (powers * inverse).astype(jnp.bfloat16)
        own_weight = (own_power * inverse).astype(jnp.bfloat16).astype(jnp.float32)
        if head == 0:
            for copy in copies[4:7]:
                copy.wait()
        values = value_ref[:, :, lanes].reshape(rows * span, HEAD)
        mixed = jnp.dot(attention, values, preferred_element_type=jnp.float32)
        new_value = jnp.concatenate([new_value_ref[:, lanes].astype(jnp.float32)] * group, 0)
        mixed = mixed + own_weight * new_value
        for member, q in enumerate(wanted):
            cols = pl.ds(q * HEAD, HEAD)
            part = hidden_ref[:, cols].astype(jnp.float32) + mixed[
                member * rows : (member + 1) * rows
            ]
            residual_ref[:, cols] = part
            total = total + jnp.sum(part, -1, keepdims=True)
    centre = total * (1.0 / feat_width)
    spread = jnp.zeros((rows, 1), jnp.float32)
    wide = 1024
    for at in range(0, feat_width, wide):
        centered = residual_ref[:, at : at + wide] - centre
        spread = spread + jnp.sum(centered * centered, -1, keepdims=True)
    inverse = lax.rsqrt(spread * (1.0 / feat_width) + 1e-05)
    for at in range(0, feat_width, wide):
        centered = residual_ref[:, at : at + wide] - centre
        normed_ref[:, at : at + wide] = (centered * inverse).astype(jnp.bfloat16)

    copies[9].wait()
    copies[10].wait()
    here = here_ref[0]
    mix = probs_ref[...] / jnp.sum(probs_ref[...], 0, keepdims=True)
    above = (
        lax.broadcasted_iota(jnp.int32, (rows, rows), 0)
        < lax.broadcasted_iota(jnp.int32, (rows, rows), 1)
    ).astype(jnp.float32)
    cap = own_ref.shape[0]
    slot = lax.broadcasted_iota(jnp.int32, (cap, rows), 0).astype(jnp.float32)
    for place, label in enumerate((here, 1 - here)):
        match = ids_ref[...] == label
        weights_ref[:, place : place + 1] = column_of(
            jnp.sum(jnp.where(match, mix, 0.0), 0, keepdims=True)
        )
        chosen = jnp.max(jnp.where(match, 1.0, 0.0), 0, keepdims=True)
        rank = jnp.dot(
            jnp.broadcast_to(chosen, (cap, rows)), above, preferred_element_type=jnp.float32
        )
        picks = jnp.where(rank == slot, chosen, 0.0)
        slots_ref[place * cap : (place + 1) * cap, :] = picks
        out_ref = (own_ref, theirs_ref)[place]
        out_ref[...] = jnp.dot(
            picks.astype(jnp.bfloat16), normed_ref[...], preferred_element_type=jnp.float32
        ).astype(jnp.bfloat16)
    copies[-1].wait()


def tail_kernel(
    residual_ref, slots_ref, weights_ref, first_ref, second_ref, third_ref, back_ref, out_ref
):
    cap = back_ref.shape[0]
    own = (
        first_ref[...].astype(jnp.float32)
        + second_ref[...].astype(jnp.float32)
        + third_ref[...].astype(jnp.float32)
    ).astype(jnp.bfloat16)
    result = residual_ref[...]
    for place, block in enumerate((own, back_ref[...])):
        picks = slots_ref[place * cap : (place + 1) * cap, :].astype(jnp.bfloat16)
        result = result + weights_ref[:, place : place + 1] * lax.dot_general(
            picks, block, (((0,), (0,)), ((), ())), preferred_element_type=jnp.float32
        )
    out_ref[...] = result


def body(
    hidden_in,
    queries,
    cache_keys,
    cache_values,
    new_keys,
    new_values,
    lengths,
    expert_ids,
    gate_probs,
    w_gate,
    w_up,
    w_down,
):
    row_count = hidden_in.shape[0]
    feat_width = hidden_in.shape[1]
    cap_slots = row_count // 2
    vmem = pl.BlockSpec(memory_space=pltpu.VMEM)
    here = lax.axis_index("expert").astype(jnp.int32).reshape(1)
    arrays = (
        hidden_in,
        queries,
        cache_keys,
        cache_values,
        new_keys,
        new_values,
        lengths.reshape(1, row_count),
        expert_ids.T,
        gate_probs.T,
        w_gate[0],
    )
    residual, own, theirs, slots, weights, gate = pl.pallas_call(
        front_kernel,
        out_shape=(
            jax.ShapeDtypeStruct((row_count, feat_width), jnp.float32),
            jax.ShapeDtypeStruct((cap_slots, feat_width), jnp.bfloat16),
            jax.ShapeDtypeStruct((cap_slots, feat_width), jnp.bfloat16),
            jax.ShapeDtypeStruct((2 * cap_slots, row_count), jnp.float32),
            jax.ShapeDtypeStruct((row_count, 2), jnp.float32),
            pltpu.VMEM(w_gate.shape[1:], w_gate.dtype),
        ),
        in_specs=[pl.BlockSpec(memory_space=pltpu.SMEM)]
        + [pl.BlockSpec(memory_space=pltpu.HBM)] * len(arrays),
        out_specs=(vmem,) * 6,
        scratch_shapes=[pltpu.VMEM(array.shape, array.dtype) for array in arrays[:-1]]
        + [
            pltpu.VMEM((row_count, feat_width), jnp.bfloat16),
            pltpu.SemaphoreType.DMA((len(arrays) + 2,)),
        ],
        compiler_params=pltpu.CompilerParams(vmem_limit_bytes=16<<20),
        cost_estimate=pl.CostEstimate(
            flops=10**9, bytes_accessed=40 * 10**6, transcendentals=10**6
        ),
    )(here, *[in_hbm(array) for array in arrays])

    count = lax.axis_size("attn")
    ring = ring_of(count)
    right = [(ring[i], ring[(i + 1) % count]) for i in range(count)]
    left = [(b, a) for a, b in right]
    right_two = [(ring[i], ring[(i + 2) % count]) for i in range(count)]
    left_two = [(b, a) for a, b in right_two]
    swap = [(0, 1), (1, 0)]

    def go_right(block):
        return lax.ppermute(block, "attn", right)

    def go_left(block):
        return lax.ppermute(block, "attn", left)

    half = count // 2
    theirs = lax.ppermute(theirs, "expert", swap)
    own_r, own_l, theirs_r, theirs_l = [own], [own], [theirs], [theirs]
    for step in range(1, half):
        own_r.append(go_right(own_r[-1]))
        own_l.append(go_left(own_l[-1]))
        theirs_l.append(go_left(theirs_l[-1]))
        theirs_r.append(go_right(theirs_r[-1]))
    own_r.append(lax.ppermute(own_r[half - 2], "attn", right_two))
    theirs_l.append(lax.ppermute(theirs_l[half - 2], "attn", left_two))

    up = load(w_up[0], own_l[half - 1], 1<<20)
    down = load(w_down[0], theirs_r[half - 1], 1<<20)
    blocks = [own, theirs]
    for step in range(1, half):
        blocks += [own_r[step], own_l[step], theirs_r[step], theirs_l[step]]
    blocks += [own_r[half], theirs_l[half]]
    share = experts(jnp.concatenate(blocks), gate, up, down).reshape(len(blocks), cap_slots, feat_width)
    own_share = {0: share[0], half: share[-2]}
    theirs_share = {0: share[1], -half: share[-1]}
    for step in range(1, half):
        at = 4 * step - 2
        own_share[-step], own_share[step] = share[at], share[at + 1]
        theirs_share[-step], theirs_share[step] = share[at + 2], share[at + 3]

    own_from_l = add(
        lax.ppermute(own_share[half], "attn", right_two),
        go_right(own_share[half - 1]),
        own_share[half - 2],
    )
    theirs_from_r = add(
        lax.ppermute(theirs_share[-half], "attn", left_two),
        go_left(theirs_share[1 - half]),
        theirs_share[2 - half],
    )
    own_from_r = own_share[1 - half]
    theirs_from_l = theirs_share[half - 1]
    for step in range(half - 2, 0, -1):
        own_from_r = add(go_left(own_from_r), own_share[-step])
        theirs_from_l = add(go_right(theirs_from_l), theirs_share[step])
        if step < half - 2:
            own_from_l = add(go_right(own_from_l), own_share[step])
            theirs_from_r = add(go_left(theirs_from_r), theirs_share[-step])
    theirs_total = add(
        theirs_share[0], go_left(theirs_from_r), go_right(theirs_from_l)
    )
    back = lax.ppermute(theirs_total, "expert", swap)
    return pl.pallas_call(
        tail_kernel,
        out_shape=jax.ShapeDtypeStruct((row_count, feat_width), jnp.float32),
        in_specs=[vmem] * 7,
        out_specs=vmem,
        compiler_params=pltpu.CompilerParams(vmem_limit_bytes=4 << 20),
    )(
        residual,
        slots,
        weights,
        own_share[0],
        go_right(own_from_l),
        go_left(own_from_r),
        back,
    )


def solution(mesh):
    placed = (
        P(("groups", "attn", "expert"), None),
        P(("groups", "attn", "expert"), None),
        P(("groups", "attn", "expert"), None, None),
        P(("groups", "attn", "expert"), None, None),
        P(("groups", "attn", "expert"), None),
        P(("groups", "attn", "expert"), None),
        P(("groups", "attn", "expert")),
        P(("groups", "attn", "expert"), None),
        P(("groups", "attn", "expert"), None),
        P("expert", None, "attn"),
        P("expert", None, "attn"),
        P("expert", "attn", None),
    )
    return jax.shard_map(
        body,
        mesh=mesh,
        in_specs=placed,
        out_specs=P(("groups", "attn", "expert"), None),
        check_vma=False,
    )
```

```python
import math

import jax
import jax.numpy as jnp
from jax import lax
from jax.experimental import pallas as pl
from jax.experimental.pallas import tpu as pltpu
from jax.sharding import PartitionSpec as P

HEAD = 128


def ring_of(count):
    if count == 8:
        return [0, 2, 4, 6, 7, 5, 3, 1]
    return list(range(count))


def in_hbm(array):
    return pltpu.with_memory_space_constraint(array, pltpu.HBM)


def experts_kernel(rows_ref, gate_ref, upward_ref, act_ref):
    hidden = gate_ref.shape[1]
    step = math.gcd(hidden, 256)
    for at in range(0, hidden, step):
        columns = slice(at, at + step)
        gate_act = jnp.dot(
            rows_ref[...], gate_ref[:, columns], preferred_element_type=jnp.float32
        )
        act_ref[:, columns] = (
            gate_act / (1.0 + jnp.exp(-gate_act)) * upward_ref[:, columns]
        ).astype(act_ref.dtype)


def activate(rows, gate, upward):
    count, feat_width = rows.shape
    hidden = gate.shape[1]
    vmem = pl.BlockSpec(memory_space=pltpu.VMEM)
    return pl.pallas_call(
        experts_kernel,
        out_shape=jax.ShapeDtypeStruct((count, hidden), jnp.bfloat16),
        in_specs=[vmem] * 3,
        out_specs=vmem,
        compiler_params=pltpu.CompilerParams(vmem_limit_bytes=8 << 20),
        cost_estimate=pl.CostEstimate(
            flops=2 * count * feat_width * hidden,
            bytes_accessed=2 * feat_width * hidden,
            transcendentals=count * hidden,
        ),
    )(rows, gate, upward)


def add_kernel(*refs):
    total = refs[0][...].astype(jnp.float32)
    for ref in refs[1:-1]:
        total = total + ref[...].astype(jnp.float32)
    refs[-1][...] = total.astype(refs[-1].dtype)


def add(*terms):
    vmem = pl.BlockSpec(memory_space=pltpu.VMEM)
    size = terms[0].size
    return pl.pallas_call(
        add_kernel,
        out_shape=jax.ShapeDtypeStruct(terms[0].shape, terms[0].dtype),
        in_specs=[vmem] * len(terms),
        out_specs=vmem,
        compiler_params=pltpu.CompilerParams(vmem_limit_bytes=1 << 20),
        cost_estimate=pl.CostEstimate(
            flops=size * len(terms), bytes_accessed=2 * size * len(terms), transcendentals=0
        ),
    )(*terms)


def column_of(row):
    shape = (row.shape[1], row.shape[1])
    same = lax.broadcasted_iota(jnp.int32, shape, 0) == lax.broadcasted_iota(jnp.int32, shape, 1)
    return jnp.sum(jnp.where(same, row, 0.0), -1, keepdims=True)


def front_kernel(
    here_ref,
    hidden_hbm,
    query_hbm,
    key_hbm,
    value_hbm,
    new_key_hbm,
    new_value_hbm,
    length_hbm,
    ids_hbm,
    probs_hbm,
    gate_hbm,
    residual_ref,
    own_ref,
    theirs_ref,
    slots_ref,
    weights_ref,
    gate_ref,
    hidden_ref,
    query_ref,
    key_ref,
    value_ref,
    new_key_ref,
    new_value_ref,
    length_ref,
    ids_ref,
    probs_ref,
    normed_ref,
    sems,
):
    half = key_ref.shape[2] // 2
    low, high = pl.ds(0, half), pl.ds(half, half)
    pairs = [
        (length_hbm, length_ref),
        (query_hbm, query_ref),
        (key_hbm.at[:, :, low], key_ref.at[:, :, low]),
        (new_key_hbm, new_key_ref),
        (value_hbm.at[:, :, low], value_ref.at[:, :, low]),
        (new_value_hbm, new_value_ref),
        (hidden_hbm, hidden_ref),
        (key_hbm.at[:, :, high], key_ref.at[:, :, high]),
        (value_hbm.at[:, :, high], value_ref.at[:, :, high]),
        (ids_hbm, ids_ref),
        (probs_hbm, probs_ref),
        (gate_hbm, gate_ref),
    ]
    copies = [
        pltpu.make_async_copy(source, target, sems.at[at])
        for at, (source, target) in enumerate(pairs)
    ]
    for copy in copies[:-1]:
        copy.start()
    for copy in copies[:4]:
        copy.wait()
    copies[-1].start()
    rows, feat_width = hidden_ref.shape
    span = key_ref.shape[1]
    kv_width = key_ref.shape[2]
    kv_heads = kv_width // HEAD
    group = feat_width // kv_width
    scale = 1.0 / math.sqrt(HEAD)
    shape = (group * rows, rows * span)
    column = lax.broadcasted_iota(jnp.int32, shape, 1)
    request = lax.broadcasted_iota(jnp.int32, shape, 0) & (rows - 1)
    first = request * span
    lengths = column_of(length_ref[...].astype(jnp.float32)).astype(jnp.int32)
    limit = first + jnp.concatenate([lengths] * group, 0)
    valid = (column >= first) & (column < limit)
    total = jnp.zeros((rows, 1), jnp.float32)
    for head in range(kv_heads):
        if head * 2 == kv_heads:
            copies[7].wait()
            copies[8].wait()
        lanes = pl.ds(head * HEAD, HEAD)
        wanted = [head * group + member for member in range(group)]
        query = jnp.concatenate([query_ref[:, q * HEAD : (q + 1) * HEAD] for q in wanted], 0)
        keys = key_ref[:, :, lanes].reshape(rows * span, HEAD)
        scores = (
            lax.dot_general(
                query, keys, (((1,), (1,)), ((), ())), preferred_element_type=jnp.float32
            )
            * scale
        )
        scores = jnp.where(valid, scores, -1e30)
        new_key = jnp.concatenate([new_key_ref[:, lanes].astype(jnp.float32)] * group, 0)
        own_score = jnp.sum(query.astype(jnp.float32) * new_key, -1, keepdims=True) * scale
        top = jnp.maximum(jnp.max(scores, -1, keepdims=True), own_score)
        powers = jnp.exp(scores - top)
        own_power = jnp.exp(own_score - top)
        inverse = 1.0 / (jnp.sum(powers, -1, keepdims=True) + own_power)
        attention = (powers * inverse).astype(jnp.bfloat16)
        own_weight = (own_power * inverse).astype(jnp.bfloat16).astype(jnp.float32)
        if head == 0:
            for copy in copies[4:7]:
                copy.wait()
        values = value_ref[:, :, lanes].reshape(rows * span, HEAD)
        mixed = jnp.dot(attention, values, preferred_element_type=jnp.float32)
        new_value = jnp.concatenate([new_value_ref[:, lanes].astype(jnp.float32)] * group, 0)
        mixed = mixed + own_weight * new_value
        for member, q in enumerate(wanted):
            cols = pl.ds(q * HEAD, HEAD)
            part = hidden_ref[:, cols].astype(jnp.float32) + mixed[
                member * rows : (member + 1) * rows
            ]
            residual_ref[:, cols] = part
            total = total + jnp.sum(part, -1, keepdims=True)
    centre = total * (1.0 / feat_width)
    spread = jnp.zeros((rows, 1), jnp.float32)
    wide = 1024
    for at in range(0, feat_width, wide):
        centered = residual_ref[:, at : at + wide] - centre
        spread = spread + jnp.sum(centered * centered, -1, keepdims=True)
    inverse = lax.rsqrt(spread * (1.0 / feat_width) + 1e-05)
    for at in range(0, feat_width, wide):
        centered = residual_ref[:, at : at + wide] - centre
        normed_ref[:, at : at + wide] = (centered * inverse).astype(jnp.bfloat16)

    copies[9].wait()
    copies[10].wait()
    here = here_ref[0]
    mix = probs_ref[...] / jnp.sum(probs_ref[...], 0, keepdims=True)
    above = (
        lax.broadcasted_iota(jnp.int32, (rows, rows), 0)
        < lax.broadcasted_iota(jnp.int32, (rows, rows), 1)
    ).astype(jnp.float32)
    cap = own_ref.shape[0]
    slot = lax.broadcasted_iota(jnp.int32, (cap, rows), 0).astype(jnp.float32)
    for place, label in enumerate((here, 1 - here)):
        match = ids_ref[...] == label
        weights_ref[:, place : place + 1] = column_of(
            jnp.sum(jnp.where(match, mix, 0.0), 0, keepdims=True)
        )
        chosen = jnp.max(jnp.where(match, 1.0, 0.0), 0, keepdims=True)
        rank = jnp.dot(
            jnp.broadcast_to(chosen, (cap, rows)), above, preferred_element_type=jnp.float32
        )
        picks = jnp.where(rank == slot, chosen, 0.0)
        slots_ref[place * cap : (place + 1) * cap, :] = picks
        out_ref = (own_ref, theirs_ref)[place]
        out_ref[...] = jnp.dot(
            picks.astype(jnp.bfloat16), normed_ref[...], preferred_element_type=jnp.float32
        ).astype(jnp.bfloat16)
    copies[-1].wait()


def tail_kernel(
    residual_ref, slots_ref, weights_ref, first_ref, second_ref, third_ref, back_ref, out_ref
):
    cap = back_ref.shape[0]
    own = (
        first_ref[...].astype(jnp.float32)
        + second_ref[...].astype(jnp.float32)
        + third_ref[...].astype(jnp.float32)
    ).astype(jnp.bfloat16)
    result = residual_ref[...]
    for place, block in enumerate((own, back_ref[...])):
        picks = slots_ref[place * cap : (place + 1) * cap, :].astype(jnp.bfloat16)
        result = result + weights_ref[:, place : place + 1] * lax.dot_general(
            picks, block, (((0,), (0,)), ((), ())), preferred_element_type=jnp.float32
        )
    out_ref[...] = result


def body(
    hidden_in,
    queries,
    cache_keys,
    cache_values,
    new_keys,
    new_values,
    lengths,
    expert_ids,
    gate_probs,
    w_gate,
    w_up,
    w_down,
):
    row_count = hidden_in.shape[0]
    feat_width = hidden_in.shape[1]
    cap_slots = row_count // 2
    vmem = pl.BlockSpec(memory_space=pltpu.VMEM)
    here = lax.axis_index("expert").astype(jnp.int32).reshape(1)
    arrays = (
        hidden_in,
        queries,
        cache_keys,
        cache_values,
        new_keys,
        new_values,
        lengths.reshape(1, row_count),
        expert_ids.T,
        gate_probs.T,
        w_gate[0],
    )
    residual, own, theirs, slots, weights, gate = pl.pallas_call(
        front_kernel,
        out_shape=(
            jax.ShapeDtypeStruct((row_count, feat_width), jnp.float32),
            jax.ShapeDtypeStruct((cap_slots, feat_width), jnp.bfloat16),
            jax.ShapeDtypeStruct((cap_slots, feat_width), jnp.bfloat16),
            jax.ShapeDtypeStruct((2 * cap_slots, row_count), jnp.float32),
            jax.ShapeDtypeStruct((row_count, 2), jnp.float32),
            pltpu.VMEM(w_gate.shape[1:], w_gate.dtype),
        ),
        in_specs=[pl.BlockSpec(memory_space=pltpu.SMEM)]
        + [pl.BlockSpec(memory_space=pltpu.HBM)] * len(arrays),
        out_specs=(vmem,) * 6,
        scratch_shapes=[pltpu.VMEM(array.shape, array.dtype) for array in arrays[:-1]]
        + [
            pltpu.VMEM((row_count, feat_width), jnp.bfloat16),
            pltpu.SemaphoreType.DMA((len(arrays) + 2,)),
        ],
        compiler_params=pltpu.CompilerParams(vmem_limit_bytes=16<<20),
        cost_estimate=pl.CostEstimate(
            flops=10**9, bytes_accessed=40 * 10**6, transcendentals=10**6
        ),
    )(here, *[in_hbm(array) for array in arrays])

    count = lax.axis_size("attn")
    ring = ring_of(count)
    right = [(ring[i], ring[(i + 1) % count]) for i in range(count)]
    left = [(b, a) for a, b in right]
    right_two = [(ring[i], ring[(i + 2) % count]) for i in range(count)]
    left_two = [(b, a) for a, b in right_two]
    swap = [(0, 1), (1, 0)]

    def go_right(block):
        return lax.ppermute(block, "attn", right)

    def go_left(block):
        return lax.ppermute(block, "attn", left)

    half = count // 2
    theirs = lax.ppermute(theirs, "expert", swap)
    own_r, own_l, theirs_r, theirs_l = [own], [own], [theirs], [theirs]
    for step in range(1, half + 1):
        own_r.append(go_right(own_r[-1]))
        if step < half:
            own_l.append(go_left(own_l[-1]))
            theirs_r.append(go_right(theirs_r[-1]))
            theirs_l.append(go_left(theirs_l[-1]))
    theirs_l.append(lax.ppermute(theirs_l[half - 2], "attn", left_two))

    blocks = [own, theirs]
    for step in range(1, half):
        blocks += [own_r[step], own_l[step], theirs_r[step], theirs_l[step]]
    blocks += [own_r[half], theirs_l[half]]
    rows = jnp.concatenate(blocks)
    upward = jnp.dot(rows, w_up[0], preferred_element_type=jnp.float32)
    active = activate(rows, gate, upward)
    share = jnp.dot(active, w_down[0], preferred_element_type=jnp.float32)
    share = share.astype(jnp.bfloat16).reshape(len(blocks), cap_slots, feat_width)
    own_share = {0: share[0], half: share[-2]}
    theirs_share = {0: share[1], -half: share[-1]}
    for step in range(1, half):
        at = 4 * step - 2
        own_share[-step], own_share[step] = share[at], share[at + 1]
        theirs_share[-step], theirs_share[step] = share[at + 2], share[at + 3]

    own_from_l = own_share[half]
    theirs_from_r = theirs_share[-half]
    own_from_r = own_share[1 - half]
    theirs_from_l = theirs_share[half - 1]
    for step in range(half - 1, 0, -1):
        own_from_l = add(go_right(own_from_l), own_share[step])
        theirs_from_r = add(go_left(theirs_from_r), theirs_share[-step])
        if step > 1:
            own_from_r = add(go_left(own_from_r), own_share[1 - step])
            theirs_from_l = add(go_right(theirs_from_l), theirs_share[step - 1])
    theirs_total = add(
        theirs_share[0], go_left(theirs_from_r), go_right(theirs_from_l)
    )
    back = lax.ppermute(theirs_total, "expert", swap)
    return pl.pallas_call(
        tail_kernel,
        out_shape=jax.ShapeDtypeStruct((row_count, feat_width), jnp.float32),
        in_specs=[vmem] * 7,
        out_specs=vmem,
        compiler_params=pltpu.CompilerParams(vmem_limit_bytes=4 << 20),
    )(
        residual,
        slots,
        weights,
        own_share[0],
        go_right(own_from_l),
        go_left(own_from_r),
        back,
    )


def solution(mesh):
    placed = (
        P(("groups", "attn", "expert"), None),
        P(("groups", "attn", "expert"), None),
        P(("groups", "attn", "expert"), None, None),
        P(("groups", "attn", "expert"), None, None),
        P(("groups", "attn", "expert"), None),
        P(("groups", "attn", "expert"), None),
        P(("groups", "attn", "expert")),
        P(("groups", "attn", "expert"), None),
        P(("groups", "attn", "expert"), None),
        P("expert", None, "attn"),
        P("expert", None, "attn"),
        P("expert", "attn", None),
    )
    return jax.shard_map(
        body,
        mesh=mesh,
        in_specs=placed,
        out_specs=P(("groups", "attn", "expert"), None),
        check_vma=False,
    )
```

```python
import math

import jax
import jax.numpy as jnp
from jax import lax
from jax.experimental import pallas as pl
from jax.experimental.pallas import tpu as pltpu
from jax.sharding import PartitionSpec as P

HEAD = 128


def ring_of(count):
    if count == 8:
        return [0, 2, 4, 6, 7, 5, 3, 1]
    return list(range(count))


def in_hbm(array):
    return pltpu.with_memory_space_constraint(array, pltpu.HBM)


def load_kernel(after_ref, source_ref, held_ref, sem):
    copy = pltpu.make_async_copy(source_ref, held_ref, sem)
    copy.start()
    copy.wait()


def load(weights, after):
    return pl.pallas_call(
        load_kernel,
        out_shape=pltpu.VMEM(weights.shape, weights.dtype),
        in_specs=[pl.BlockSpec(memory_space=pl.ANY), pl.BlockSpec(memory_space=pltpu.HBM)],
        out_specs=pl.BlockSpec(memory_space=pltpu.VMEM),
        scratch_shapes=[pltpu.SemaphoreType.DMA],
        compiler_params=pltpu.CompilerParams(vmem_limit_bytes=1 << 20),
        cost_estimate=pl.CostEstimate(
            flops=0, bytes_accessed=2 * weights.size, transcendentals=0
        ),
    )(after, in_hbm(weights))


def experts_kernel(rows_ref, gate_ref, up_ref, act_ref):
    hidden = gate_ref.shape[1]
    step = math.gcd(hidden, 256)
    for at in range(0, hidden, step):
        columns = slice(at, at + step)
        gate_act = jnp.dot(
            rows_ref[...], gate_ref[:, columns], preferred_element_type=jnp.float32
        )
        upward = jnp.dot(rows_ref[...], up_ref[:, columns], preferred_element_type=jnp.float32)
        act_ref[:, columns] = (gate_act / (1.0 + jnp.exp(-gate_act)) * upward).astype(
            act_ref.dtype
        )


def activate(rows, gate, up):
    count, feat_width = rows.shape
    hidden = gate.shape[1]
    vmem = pl.BlockSpec(memory_space=pltpu.VMEM)
    return pl.pallas_call(
        experts_kernel,
        out_shape=jax.ShapeDtypeStruct((count, hidden), jnp.bfloat16),
        in_specs=[vmem] * 3,
        out_specs=vmem,
        compiler_params=pltpu.CompilerParams(vmem_limit_bytes=8 << 20),
        cost_estimate=pl.CostEstimate(
            flops=4 * count * feat_width * hidden,
            bytes_accessed=4 * feat_width * hidden,
            transcendentals=count * hidden,
        ),
    )(rows, gate, up)


def add_kernel(*refs):
    total = refs[0][...].astype(jnp.float32)
    for ref in refs[1:-1]:
        total = total + ref[...].astype(jnp.float32)
    refs[-1][...] = total.astype(refs[-1].dtype)


def add(*terms):
    vmem = pl.BlockSpec(memory_space=pltpu.VMEM)
    size = terms[0].size
    return pl.pallas_call(
        add_kernel,
        out_shape=jax.ShapeDtypeStruct(terms[0].shape, terms[0].dtype),
        in_specs=[vmem] * len(terms),
        out_specs=vmem,
        compiler_params=pltpu.CompilerParams(vmem_limit_bytes=1 << 20),
        cost_estimate=pl.CostEstimate(
            flops=size * len(terms), bytes_accessed=2 * size * len(terms), transcendentals=0
        ),
    )(*terms)


def column_of(row):
    shape = (row.shape[1], row.shape[1])
    same = lax.broadcasted_iota(jnp.int32, shape, 0) == lax.broadcasted_iota(jnp.int32, shape, 1)
    return jnp.sum(jnp.where(same, row, 0.0), -1, keepdims=True)


def front_kernel(
    here_ref,
    hidden_hbm,
    query_hbm,
    key_hbm,
    value_hbm,
    new_key_hbm,
    new_value_hbm,
    length_hbm,
    ids_hbm,
    probs_hbm,
    gate_hbm,
    residual_ref,
    own_ref,
    theirs_ref,
    slots_ref,
    weights_ref,
    gate_ref,
    hidden_ref,
    query_ref,
    key_ref,
    value_ref,
    new_key_ref,
    new_value_ref,
    length_ref,
    ids_ref,
    probs_ref,
    normed_ref,
    sems,
):
    half = key_ref.shape[2] // 2
    low, high = pl.ds(0, half), pl.ds(half, half)
    pairs = [
        (length_hbm, length_ref),
        (query_hbm, query_ref),
        (key_hbm.at[:, :, low], key_ref.at[:, :, low]),
        (new_key_hbm, new_key_ref),
        (value_hbm.at[:, :, low], value_ref.at[:, :, low]),
        (new_value_hbm, new_value_ref),
        (hidden_hbm, hidden_ref),
        (key_hbm.at[:, :, high], key_ref.at[:, :, high]),
        (value_hbm.at[:, :, high], value_ref.at[:, :, high]),
        (ids_hbm, ids_ref),
        (probs_hbm, probs_ref),
        (gate_hbm, gate_ref),
    ]
    copies = [
        pltpu.make_async_copy(source, target, sems.at[at])
        for at, (source, target) in enumerate(pairs)
    ]
    for copy in copies[:-1]:
        copy.start()
    for copy in copies[:4]:
        copy.wait()
    copies[-1].start()
    rows, feat_width = hidden_ref.shape
    span = key_ref.shape[1]
    kv_width = key_ref.shape[2]
    kv_heads = kv_width // HEAD
    group = feat_width // kv_width
    scale = math.log2(math.e) / math.sqrt(HEAD)
    eight = 8
    half_span = eight * span
    shape = (group * rows, half_span)
    column = lax.broadcasted_iota(jnp.int32, shape, 1)
    first = (lax.broadcasted_iota(jnp.int32, shape, 0) & (eight - 1)) * span
    lengths = column_of(length_ref[...].astype(jnp.float32)).astype(jnp.int32)
    limit = first + jnp.concatenate([lengths] * group, 0)
    valid = (column >= first) & (column < limit)

    def query_of(head):
        wanted = range(head * group, (head + 1) * group)
        return jnp.concatenate([query_ref[:, q * HEAD : (q + 1) * HEAD] for q in wanted], 0)

    def scores_of(head):
        if head * 2 == kv_heads:
            copies[7].wait()
            copies[8].wait()
        keys = key_ref[:, :, head * HEAD : (head + 1) * HEAD].reshape(rows * span, HEAD)
        scores = lax.dot_general(
            query_of(head), keys, (((1,), (1,)), ((), ())), preferred_element_type=jnp.float32
        )
        pieces = []
        for at in range(0, group * rows, eight):
            start = at % rows // eight * half_span
            pieces.append(scores[at : at + eight, start : start + half_span])
        return jnp.where(valid, jnp.concatenate(pieces, 0), -1e30)

    total = jnp.zeros((rows, 1), jnp.float32)
    empty = jnp.zeros((eight, half_span), jnp.float32)
    scores = scores_of(0)
    for head in range(kv_heads):
        later = scores_of(head + 1) if head + 1 < kv_heads else None
        lanes = pl.ds(head * HEAD, HEAD)
        query = query_of(head).astype(jnp.float32)
        new_key = jnp.concatenate([new_key_ref[:, lanes].astype(jnp.float32)] * group, 0)
        own_score = jnp.sum(query * new_key, -1, keepdims=True)
        top = jnp.maximum(jnp.max(scores, -1, keepdims=True), own_score)
        powers = jnp.exp2((scores - top) * scale)
        own_power = jnp.exp2((own_score - top) * scale)
        inverse = 1.0 / (jnp.sum(powers, -1, keepdims=True) + own_power)
        wide_rows = []
        for at in range(0, group * rows, eight):
            place = at % rows // eight
            parts = [empty] * (rows // eight)
            parts[place] = powers[at : at + eight]
            wide_rows.append(jnp.concatenate(parts, 1))
        attention = jnp.concatenate(wide_rows, 0).astype(jnp.bfloat16)
        if head == 0:
            for copy in copies[4:7]:
                copy.wait()
        values = value_ref[:, :, lanes].reshape(rows * span, HEAD)
        mixed = jnp.dot(attention, values, preferred_element_type=jnp.float32)
        new_value = jnp.concatenate([new_value_ref[:, lanes].astype(jnp.float32)] * group, 0)
        mixed = (mixed + own_power * new_value) * inverse
        for member in range(group):
            cols = pl.ds((head * group + member) * HEAD, HEAD)
            part = hidden_ref[:, cols].astype(jnp.float32) + mixed[
                member * rows : (member + 1) * rows
            ]
            residual_ref[:, cols] = part
            total = total + jnp.sum(part, -1, keepdims=True)
        scores = later
    centre = total * (1.0 / feat_width)
    spread = jnp.zeros((rows, 1), jnp.float32)
    wide = 1024
    for at in range(0, feat_width, wide):
        centered = residual_ref[:, at : at + wide] - centre
        spread = spread + jnp.sum(centered * centered, -1, keepdims=True)
    inverse = lax.rsqrt(spread * (1.0 / feat_width) + 1e-05)
    for at in range(0, feat_width, wide):
        centered = residual_ref[:, at : at + wide] - centre
        normed_ref[:, at : at + wide] = (centered * inverse).astype(jnp.bfloat16)

    copies[9].wait()
    copies[10].wait()
    here = here_ref[0]
    mix = probs_ref[...] / jnp.sum(probs_ref[...], 0, keepdims=True)
    above = (
        lax.broadcasted_iota(jnp.int32, (rows, rows), 0)
        < lax.broadcasted_iota(jnp.int32, (rows, rows), 1)
    ).astype(jnp.float32)
    cap = own_ref.shape[0]
    slot = lax.broadcasted_iota(jnp.int32, (cap, rows), 0).astype(jnp.float32)
    for place, label in enumerate((here, 1 - here)):
        match = ids_ref[...] == label
        weights_ref[:, place : place + 1] = column_of(
            jnp.sum(jnp.where(match, mix, 0.0), 0, keepdims=True)
        )
        chosen = jnp.max(jnp.where(match, 1.0, 0.0), 0, keepdims=True)
        rank = jnp.dot(
            jnp.broadcast_to(chosen, (cap, rows)), above, preferred_element_type=jnp.float32
        )
        picks = jnp.where(rank == slot, chosen, 0.0)
        slots_ref[place * cap : (place + 1) * cap, :] = picks
        out_ref = (own_ref, theirs_ref)[place]
        out_ref[...] = jnp.dot(
            picks.astype(jnp.bfloat16), normed_ref[...], preferred_element_type=jnp.float32
        ).astype(jnp.bfloat16)
    copies[-1].wait()


def tail_kernel(
    residual_ref,
    slots_ref,
    weights_ref,
    first_ref,
    second_ref,
    third_ref,
    back_ref,
    out_ref,
    result_ref,
    sems,
):
    cap, width = back_ref.shape
    wide = width // sems.shape[0]
    copies = []
    for at in range(sems.shape[0]):
        columns = slice(at * wide, (at + 1) * wide)
        own = (
            first_ref[:, columns].astype(jnp.float32)
            + second_ref[:, columns].astype(jnp.float32)
            + third_ref[:, columns].astype(jnp.float32)
        ).astype(jnp.bfloat16)
        result = residual_ref[:, columns]
        for place, block in enumerate((own, back_ref[:, columns])):
            picks = slots_ref[place * cap : (place + 1) * cap, :].astype(jnp.bfloat16)
            result = result + weights_ref[:, place : place + 1] * lax.dot_general(
                picks, block, (((0,), (0,)), ((), ())), preferred_element_type=jnp.float32
            )
        result_ref[:, columns] = result
        copies.append(
            pltpu.make_async_copy(
                result_ref.at[:, columns], out_ref.at[:, columns], sems.at[at]
            )
        )
        copies[-1].start()
    for copy in copies:
        copy.wait()


def body(
    hidden_in,
    queries,
    cache_keys,
    cache_values,
    new_keys,
    new_values,
    lengths,
    expert_ids,
    gate_probs,
    w_gate,
    w_up,
    w_down,
):
    row_count = hidden_in.shape[0]
    feat_width = hidden_in.shape[1]
    cap_slots = row_count // 2
    vmem = pl.BlockSpec(memory_space=pltpu.VMEM)
    here = lax.axis_index("expert").astype(jnp.int32).reshape(1)
    arrays = (
        hidden_in,
        queries,
        cache_keys,
        cache_values,
        new_keys,
        new_values,
        lengths.reshape(1, row_count),
        expert_ids.T,
        gate_probs.T,
        w_gate[0],
    )
    residual, own, theirs, slots, weights, gate = pl.pallas_call(
        front_kernel,
        out_shape=(
            jax.ShapeDtypeStruct((row_count, feat_width), jnp.float32),
            jax.ShapeDtypeStruct((cap_slots, feat_width), jnp.bfloat16),
            jax.ShapeDtypeStruct((cap_slots, feat_width), jnp.bfloat16),
            jax.ShapeDtypeStruct((2 * cap_slots, row_count), jnp.float32),
            jax.ShapeDtypeStruct((row_count, 2), jnp.float32),
            pltpu.VMEM(w_gate.shape[1:], w_gate.dtype),
        ),
        in_specs=[pl.BlockSpec(memory_space=pltpu.SMEM)]
        + [pl.BlockSpec(memory_space=pltpu.HBM)] * len(arrays),
        out_specs=(vmem,) * 6,
        scratch_shapes=[pltpu.VMEM(array.shape, array.dtype) for array in arrays[:-1]]
        + [
            pltpu.VMEM((row_count, feat_width), jnp.bfloat16),
            pltpu.SemaphoreType.DMA((len(arrays) + 2,)),
        ],
        compiler_params=pltpu.CompilerParams(vmem_limit_bytes=16<<20),
        cost_estimate=pl.CostEstimate(
            flops=10**9, bytes_accessed=40 * 10**6, transcendentals=10**6
        ),
    )(here, *[in_hbm(array) for array in arrays])

    count = lax.axis_size("attn")
    ring = ring_of(count)
    right = [(ring[i], ring[(i + 1) % count]) for i in range(count)]
    left = [(b, a) for a, b in right]
    right_two = [(ring[i], ring[(i + 2) % count]) for i in range(count)]
    left_two = [(b, a) for a, b in right_two]
    swap = [(0, 1), (1, 0)]

    def go_right(block):
        return lax.ppermute(block, "attn", right)

    def go_left(block):
        return lax.ppermute(block, "attn", left)

    half = count // 2
    theirs = lax.ppermute(theirs, "expert", swap)
    own_r, own_l, theirs_r, theirs_l = [own], [own], [theirs], [theirs]
    for step in range(1, half + 1):
        own_r.append(go_right(own_r[-1]))
        if step < half:
            own_l.append(go_left(own_l[-1]))
            theirs_r.append(go_right(theirs_r[-1]))
            theirs_l.append(go_left(theirs_l[-1]))
    theirs_l.append(lax.ppermute(theirs_l[half - 2], "attn", left_two))

    up = load(w_up[0], theirs_r[half - 2])
    blocks = [own, theirs]
    for step in range(1, half):
        blocks += [own_r[step], own_l[step], theirs_r[step], theirs_l[step]]
    blocks += [own_r[half], theirs_l[half]]
    rows = jnp.concatenate(blocks)
    active = activate(rows, gate, up)
    share = jnp.dot(active, w_down[0], preferred_element_type=jnp.float32)
    share = share.astype(jnp.bfloat16).reshape(len(blocks), cap_slots, feat_width)
    own_share = {0: share[0], half: share[-2]}
    theirs_share = {0: share[1], -half: share[-1]}
    for step in range(1, half):
        at = 4 * step - 2
        own_share[-step], own_share[step] = share[at], share[at + 1]
        theirs_share[-step], theirs_share[step] = share[at + 2], share[at + 3]

    own_from_l = own_share[half]
    theirs_from_r = theirs_share[-half]
    own_from_r = own_share[1 - half]
    theirs_from_l = theirs_share[half - 1]
    for step in range(half - 1, 0, -1):
        own_from_l = add(go_right(own_from_l), own_share[step])
        theirs_from_r = add(go_left(theirs_from_r), theirs_share[-step])
        if step > 1:
            own_from_r = add(go_left(own_from_r), own_share[1 - step])
            theirs_from_l = add(go_right(theirs_from_l), theirs_share[step - 1])
    theirs_total = add(
        theirs_share[0], go_left(theirs_from_r), go_right(theirs_from_l)
    )
    back = lax.ppermute(theirs_total, "expert", swap)
    return pl.pallas_call(
        tail_kernel,
        out_shape=jax.ShapeDtypeStruct((row_count, feat_width), jnp.float32),
        in_specs=[vmem] * 7,
        out_specs=pl.BlockSpec(memory_space=pltpu.HBM),
        scratch_shapes=[
            pltpu.VMEM((row_count, feat_width), jnp.float32),
            pltpu.SemaphoreType.DMA((4,)),
        ],
        compiler_params=pltpu.CompilerParams(vmem_limit_bytes=4 << 20),
    )(
        residual,
        slots,
        weights,
        own_share[0],
        go_right(own_from_l),
        go_left(own_from_r),
        back,
    )


def solution(mesh):
    placed = (
        P(("groups", "attn", "expert"), None),
        P(("groups", "attn", "expert"), None),
        P(("groups", "attn", "expert"), None, None),
        P(("groups", "attn", "expert"), None, None),
        P(("groups", "attn", "expert"), None),
        P(("groups", "attn", "expert"), None),
        P(("groups", "attn", "expert")),
        P(("groups", "attn", "expert"), None),
        P(("groups", "attn", "expert"), None),
        P("expert", None, "attn"),
        P("expert", None, "attn"),
        P("expert", "attn", None),
    )
    return jax.shard_map(
        body,
        mesh=mesh,
        in_specs=placed,
        out_specs=P(("groups", "attn", "expert"), None),
        check_vma=False,
    )
```

```python
import math

import jax
import jax.numpy as jnp
from jax import lax
from jax.experimental import pallas as pl
from jax.experimental.pallas import tpu as pltpu
from jax.sharding import PartitionSpec as P

HEAD = 128


def ring_of(count):
    if count == 8:
        return [0, 2, 4, 6, 7, 5, 3, 1]
    return list(range(count))


def in_hbm(array):
    return pltpu.with_memory_space_constraint(array, pltpu.HBM)


def load_kernel(after_ref, source_ref, held_ref, sem):
    copy = pltpu.make_async_copy(source_ref, held_ref, sem)
    copy.start()
    copy.wait()


def load(weights, after):
    return pl.pallas_call(
        load_kernel,
        out_shape=pltpu.VMEM(weights.shape, weights.dtype),
        in_specs=[pl.BlockSpec(memory_space=pl.ANY), pl.BlockSpec(memory_space=pltpu.HBM)],
        out_specs=pl.BlockSpec(memory_space=pltpu.VMEM),
        scratch_shapes=[pltpu.SemaphoreType.DMA],
        compiler_params=pltpu.CompilerParams(vmem_limit_bytes=1 << 20),
        cost_estimate=pl.CostEstimate(
            flops=0, bytes_accessed=2 * weights.size, transcendentals=0
        ),
    )(after, in_hbm(weights))


def experts_kernel(rows_ref, gate_ref, up_ref, act_ref):
    hidden = gate_ref.shape[1]
    step = math.gcd(hidden, 256)
    for at in range(0, hidden, step):
        columns = slice(at, at + step)
        gate_act = jnp.dot(
            rows_ref[...], gate_ref[:, columns], preferred_element_type=jnp.float32
        )
        upward = jnp.dot(rows_ref[...], up_ref[:, columns], preferred_element_type=jnp.float32)
        act_ref[:, columns] = (gate_act / (1.0 + jnp.exp(-gate_act)) * upward).astype(
            act_ref.dtype
        )


def activate(rows, gate, up):
    count, feat_width = rows.shape
    hidden = gate.shape[1]
    vmem = pl.BlockSpec(memory_space=pltpu.VMEM)
    return pl.pallas_call(
        experts_kernel,
        out_shape=jax.ShapeDtypeStruct((count, hidden), jnp.bfloat16),
        in_specs=[vmem] * 3,
        out_specs=vmem,
        compiler_params=pltpu.CompilerParams(vmem_limit_bytes=8 << 20),
        cost_estimate=pl.CostEstimate(
            flops=4 * count * feat_width * hidden,
            bytes_accessed=4 * feat_width * hidden,
            transcendentals=count * hidden,
        ),
    )(rows, gate, up)


def add_kernel(*refs):
    total = refs[0][...].astype(jnp.float32)
    for ref in refs[1:-1]:
        total = total + ref[...].astype(jnp.float32)
    refs[-1][...] = total.astype(refs[-1].dtype)


def add(*terms):
    vmem = pl.BlockSpec(memory_space=pltpu.VMEM)
    size = terms[0].size
    return pl.pallas_call(
        add_kernel,
        out_shape=jax.ShapeDtypeStruct(terms[0].shape, terms[0].dtype),
        in_specs=[vmem] * len(terms),
        out_specs=vmem,
        compiler_params=pltpu.CompilerParams(vmem_limit_bytes=1 << 20),
        cost_estimate=pl.CostEstimate(
            flops=size * len(terms), bytes_accessed=2 * size * len(terms), transcendentals=0
        ),
    )(*terms)


def column_of(row):
    shape = (row.shape[1], row.shape[1])
    same = lax.broadcasted_iota(jnp.int32, shape, 0) == lax.broadcasted_iota(jnp.int32, shape, 1)
    return jnp.sum(jnp.where(same, row, 0.0), -1, keepdims=True)


def front_kernel(
    here_ref,
    hidden_hbm,
    query_hbm,
    key_hbm,
    value_hbm,
    new_key_hbm,
    new_value_hbm,
    length_hbm,
    ids_hbm,
    probs_hbm,
    gate_hbm,
    residual_ref,
    own_ref,
    theirs_ref,
    slots_ref,
    weights_ref,
    gate_ref,
    hidden_ref,
    query_ref,
    key_ref,
    value_ref,
    new_key_ref,
    new_value_ref,
    length_ref,
    ids_ref,
    probs_ref,
    normed_ref,
    sems,
):
    half = key_ref.shape[2] // 2
    low, high = pl.ds(0, half), pl.ds(half, half)
    pairs = [
        (length_hbm, length_ref),
        (query_hbm, query_ref),
        (key_hbm.at[:, :, low], key_ref.at[:, :, low]),
        (new_key_hbm, new_key_ref),
        (value_hbm.at[:, :, low], value_ref.at[:, :, low]),
        (new_value_hbm, new_value_ref),
        (hidden_hbm, hidden_ref),
        (key_hbm.at[:, :, high], key_ref.at[:, :, high]),
        (value_hbm.at[:, :, high], value_ref.at[:, :, high]),
        (ids_hbm, ids_ref),
        (probs_hbm, probs_ref),
        (gate_hbm, gate_ref),
    ]
    copies = [
        pltpu.make_async_copy(source, target, sems.at[at])
        for at, (source, target) in enumerate(pairs)
    ]
    for copy in copies[:-1]:
        copy.start()
    for copy in copies[:4]:
        copy.wait()
    copies[-1].start()
    rows, feat_width = hidden_ref.shape
    span = key_ref.shape[1]
    kv_width = key_ref.shape[2]
    kv_heads = kv_width // HEAD
    group = feat_width // kv_width
    scale = math.log2(math.e) / math.sqrt(HEAD)
    eight = 8
    half_span = eight * span
    shape = (group * rows, half_span)
    column = lax.broadcasted_iota(jnp.int32, shape, 1)
    first = (lax.broadcasted_iota(jnp.int32, shape, 0) & (eight - 1)) * span
    lengths = column_of(length_ref[...].astype(jnp.float32)).astype(jnp.int32)
    limit = first + jnp.concatenate([lengths] * group, 0)
    valid = (column >= first) & (column < limit)

    def query_of(head):
        wanted = range(head * group, (head + 1) * group)
        return jnp.concatenate([query_ref[:, q * HEAD : (q + 1) * HEAD] for q in wanted], 0)

    def scores_of(head):
        if head * 2 == kv_heads:
            copies[7].wait()
            copies[8].wait()
        keys = key_ref[:, :, head * HEAD : (head + 1) * HEAD].reshape(rows * span, HEAD)
        scores = lax.dot_general(
            query_of(head), keys, (((1,), (1,)), ((), ())), preferred_element_type=jnp.float32
        )
        pieces = []
        for at in range(0, group * rows, eight):
            start = at % rows // eight * half_span
            pieces.append(scores[at : at + eight, start : start + half_span])
        return jnp.where(valid, jnp.concatenate(pieces, 0), -1e30)

    total = jnp.zeros((rows, 1), jnp.float32)
    empty = jnp.zeros((eight, half_span), jnp.float32)
    scores = scores_of(0)
    for head in range(kv_heads):
        later = scores_of(head + 1) if head + 1 < kv_heads else None
        lanes = pl.ds(head * HEAD, HEAD)
        query = query_of(head).astype(jnp.float32)
        new_key = jnp.concatenate([new_key_ref[:, lanes].astype(jnp.float32)] * group, 0)
        own_score = jnp.sum(query * new_key, -1, keepdims=True)
        top = jnp.maximum(jnp.max(scores, -1, keepdims=True), own_score)
        powers = jnp.exp2((scores - top) * scale)
        own_power = jnp.exp2((own_score - top) * scale)
        inverse = 1.0 / (jnp.sum(powers, -1, keepdims=True) + own_power)
        powers = powers * inverse
        own_weight = (own_power * inverse).astype(jnp.bfloat16).astype(jnp.float32)
        wide_rows = []
        for at in range(0, group * rows, eight):
            place = at % rows // eight
            parts = [empty] * (rows // eight)
            parts[place] = powers[at : at + eight]
            wide_rows.append(jnp.concatenate(parts, 1))
        attention = jnp.concatenate(wide_rows, 0).astype(jnp.bfloat16)
        if head == 0:
            for copy in copies[4:7]:
                copy.wait()
        values = value_ref[:, :, lanes].reshape(rows * span, HEAD)
        mixed = jnp.dot(attention, values, preferred_element_type=jnp.float32)
        new_value = jnp.concatenate([new_value_ref[:, lanes].astype(jnp.float32)] * group, 0)
        mixed = mixed + own_weight * new_value
        for member in range(group):
            cols = pl.ds((head * group + member) * HEAD, HEAD)
            part = hidden_ref[:, cols].astype(jnp.float32) + mixed[
                member * rows : (member + 1) * rows
            ]
            residual_ref[:, cols] = part
            total = total + jnp.sum(part, -1, keepdims=True)
        scores = later
    centre = total * (1.0 / feat_width)
    spread = jnp.zeros((rows, 1), jnp.float32)
    wide = 1024
    for at in range(0, feat_width, wide):
        centered = residual_ref[:, at : at + wide] - centre
        spread = spread + jnp.sum(centered * centered, -1, keepdims=True)
    inverse = lax.rsqrt(spread * (1.0 / feat_width) + 1e-05)
    for at in range(0, feat_width, wide):
        centered = residual_ref[:, at : at + wide] - centre
        normed_ref[:, at : at + wide] = (centered * inverse).astype(jnp.bfloat16)

    copies[9].wait()
    copies[10].wait()
    here = here_ref[0]
    mix = probs_ref[...] / jnp.sum(probs_ref[...], 0, keepdims=True)
    above = (
        lax.broadcasted_iota(jnp.int32, (rows, rows), 0)
        < lax.broadcasted_iota(jnp.int32, (rows, rows), 1)
    ).astype(jnp.float32)
    cap = own_ref.shape[0]
    slot = lax.broadcasted_iota(jnp.int32, (cap, rows), 0).astype(jnp.float32)
    for place, label in enumerate((here, 1 - here)):
        match = ids_ref[...] == label
        weights_ref[:, place : place + 1] = column_of(
            jnp.sum(jnp.where(match, mix, 0.0), 0, keepdims=True)
        )
        chosen = jnp.max(jnp.where(match, 1.0, 0.0), 0, keepdims=True)
        rank = jnp.dot(
            jnp.broadcast_to(chosen, (cap, rows)), above, preferred_element_type=jnp.float32
        )
        picks = jnp.where(rank == slot, chosen, 0.0)
        slots_ref[place * cap : (place + 1) * cap, :] = picks
        out_ref = (own_ref, theirs_ref)[place]
        out_ref[...] = jnp.dot(
            picks.astype(jnp.bfloat16), normed_ref[...], preferred_element_type=jnp.float32
        ).astype(jnp.bfloat16)
    copies[-1].wait()


def tail_kernel(
    residual_ref,
    slots_ref,
    weights_ref,
    first_ref,
    second_ref,
    third_ref,
    back_ref,
    out_ref,
    result_ref,
    sems,
):
    cap, width = back_ref.shape
    wide = width // sems.shape[0]
    copies = []
    for at in range(sems.shape[0]):
        columns = slice(at * wide, (at + 1) * wide)
        own = (
            first_ref[:, columns].astype(jnp.float32)
            + second_ref[:, columns].astype(jnp.float32)
            + third_ref[:, columns].astype(jnp.float32)
        ).astype(jnp.bfloat16)
        result = residual_ref[:, columns]
        for place, block in enumerate((own, back_ref[:, columns])):
            picks = slots_ref[place * cap : (place + 1) * cap, :].astype(jnp.bfloat16)
            result = result + weights_ref[:, place : place + 1] * lax.dot_general(
                picks, block, (((0,), (0,)), ((), ())), preferred_element_type=jnp.float32
            )
        result_ref[:, columns] = result
        copies.append(
            pltpu.make_async_copy(
                result_ref.at[:, columns], out_ref.at[:, columns], sems.at[at]
            )
        )
        copies[-1].start()
    for copy in copies:
        copy.wait()


def body(
    hidden_in,
    queries,
    cache_keys,
    cache_values,
    new_keys,
    new_values,
    lengths,
    expert_ids,
    gate_probs,
    w_gate,
    w_up,
    w_down,
):
    row_count = hidden_in.shape[0]
    feat_width = hidden_in.shape[1]
    cap_slots = row_count // 2
    vmem = pl.BlockSpec(memory_space=pltpu.VMEM)
    here = lax.axis_index("expert").astype(jnp.int32).reshape(1)
    arrays = (
        hidden_in,
        queries,
        cache_keys,
        cache_values,
        new_keys,
        new_values,
        lengths.reshape(1, row_count),
        expert_ids.T,
        gate_probs.T,
        w_gate[0],
    )
    residual, own, theirs, slots, weights, gate = pl.pallas_call(
        front_kernel,
        out_shape=(
            jax.ShapeDtypeStruct((row_count, feat_width), jnp.float32),
            jax.ShapeDtypeStruct((cap_slots, feat_width), jnp.bfloat16),
            jax.ShapeDtypeStruct((cap_slots, feat_width), jnp.bfloat16),
            jax.ShapeDtypeStruct((2 * cap_slots, row_count), jnp.float32),
            jax.ShapeDtypeStruct((row_count, 2), jnp.float32),
            pltpu.VMEM(w_gate.shape[1:], w_gate.dtype),
        ),
        in_specs=[pl.BlockSpec(memory_space=pltpu.SMEM)]
        + [pl.BlockSpec(memory_space=pltpu.HBM)] * len(arrays),
        out_specs=(vmem,) * 6,
        scratch_shapes=[pltpu.VMEM(array.shape, array.dtype) for array in arrays[:-1]]
        + [
            pltpu.VMEM((row_count, feat_width), jnp.bfloat16),
            pltpu.SemaphoreType.DMA((len(arrays) + 2,)),
        ],
        compiler_params=pltpu.CompilerParams(vmem_limit_bytes=16<<20),
        cost_estimate=pl.CostEstimate(
            flops=10**9, bytes_accessed=40 * 10**6, transcendentals=10**6
        ),
    )(here, *[in_hbm(array) for array in arrays])

    count = lax.axis_size("attn")
    ring = ring_of(count)
    right = [(ring[i], ring[(i + 1) % count]) for i in range(count)]
    left = [(b, a) for a, b in right]
    right_two = [(ring[i], ring[(i + 2) % count]) for i in range(count)]
    left_two = [(b, a) for a, b in right_two]
    swap = [(0, 1), (1, 0)]

    def go_right(block):
        return lax.ppermute(block, "attn", right)

    def go_left(block):
        return lax.ppermute(block, "attn", left)

    half = count // 2
    theirs = lax.ppermute(theirs, "expert", swap)
    own_r, own_l, theirs_r, theirs_l = [own], [own], [theirs], [theirs]
    for step in range(1, half + 1):
        own_r.append(go_right(own_r[-1]))
        if step < half:
            own_l.append(go_left(own_l[-1]))
            theirs_r.append(go_right(theirs_r[-1]))
            theirs_l.append(go_left(theirs_l[-1]))
    theirs_l.append(lax.ppermute(theirs_l[half - 2], "attn", left_two))

    up = load(w_up[0], theirs_r[half - 2])
    blocks = [own, theirs]
    for step in range(1, half):
        blocks += [own_r[step], own_l[step], theirs_r[step], theirs_l[step]]
    blocks += [own_r[half], theirs_l[half]]
    rows = jnp.concatenate(blocks)
    active = activate(rows, gate, up)
    share = jnp.dot(active, w_down[0], preferred_element_type=jnp.float32)
    share = share.astype(jnp.bfloat16).reshape(len(blocks), cap_slots, feat_width)
    own_share = {0: share[0], half: share[-2]}
    theirs_share = {0: share[1], -half: share[-1]}
    for step in range(1, half):
        at = 4 * step - 2
        own_share[-step], own_share[step] = share[at], share[at + 1]
        theirs_share[-step], theirs_share[step] = share[at + 2], share[at + 3]

    own_from_l = own_share[half]
    theirs_from_r = theirs_share[-half]
    own_from_r = own_share[1 - half]
    theirs_from_l = theirs_share[half - 1]
    for step in range(half - 1, 0, -1):
        from_l, from_r = go_right(own_from_l), go_left(theirs_from_r)
        if step == half - 1:
            own_from_r, _ = lax.optimization_barrier((own_from_r, from_l))
        own_from_l = add(from_l, own_share[step])
        theirs_from_r = add(from_r, theirs_share[-step])
        if step > 1:
            own_from_r = add(go_left(own_from_r), own_share[1 - step])
            theirs_from_l = add(go_right(theirs_from_l), theirs_share[step - 1])
    theirs_total = add(
        theirs_share[0], go_left(theirs_from_r), go_right(theirs_from_l)
    )
    back = lax.ppermute(theirs_total, "expert", swap)
    return pl.pallas_call(
        tail_kernel,
        out_shape=jax.ShapeDtypeStruct((row_count, feat_width), jnp.float32),
        in_specs=[vmem] * 7,
        out_specs=pl.BlockSpec(memory_space=pltpu.HBM),
        scratch_shapes=[
            pltpu.VMEM((row_count, feat_width), jnp.float32),
            pltpu.SemaphoreType.DMA((4,)),
        ],
        compiler_params=pltpu.CompilerParams(vmem_limit_bytes=4 << 20),
    )(
        residual,
        slots,
        weights,
        own_share[0],
        go_right(own_from_l),
        go_left(own_from_r),
        back,
    )


def solution(mesh):
    placed = (
        P(("groups", "attn", "expert"), None),
        P(("groups", "attn", "expert"), None),
        P(("groups", "attn", "expert"), None, None),
        P(("groups", "attn", "expert"), None, None),
        P(("groups", "attn", "expert"), None),
        P(("groups", "attn", "expert"), None),
        P(("groups", "attn", "expert")),
        P(("groups", "attn", "expert"), None),
        P(("groups", "attn", "expert"), None),
        P("expert", None, "attn"),
        P("expert", None, "attn"),
        P("expert", "attn", None),
    )
    return jax.shard_map(
        body,
        mesh=mesh,
        in_specs=placed,
        out_specs=P(("groups", "attn", "expert"), None),
        check_vma=False,
    )
```
